512 devices in a mesh: ctx: 64 (over x_hi, z, core), tp: 8 (over y, x_lo).
Axes of the slice: x: 4 (x_hi: 2, x_lo: 2; x = x_hi * 2 + x_lo), y: 4, z: 16, core: 2. Of those that a mesh axis runs over, the one named last changes fastest.
Arguments:
- queries: bfloat16 [14336, 5120], P('ctx', 'tp'), may hold values from -8 to 8
- keys: bfloat16 [14336, 1024], P('ctx', 'tp'), may hold values from -8 to 8
- values: bfloat16 [14336, 1024], P('ctx', 'tp'), may hold values from -6 to 6
- doc_lengths: int32 [16], replicated, may hold values from 1 to 7168, 14336 in all
- out_weight: bfloat16 [40, 128, 5120], P('tp', 'ctx'), may hold values from -0.83984375 to 0.83984375
Outputs:
- attended: float32 [14336, 5120], P('ctx', 'tp')
- projected: float32 [14336, 5120], P('ctx', 'tp')
The draws below stay inside these ranges and needn't reach their ends.
Inputs may be any that keep to these rules, and one draw needn't show every extreme that they name: `doc_lengths`: the 16 lengths sum to 14336; the longest document has exactly 7168 positions.
All inputs are finite; a program needn't handle non-finite values.
Results may differ from the reference program's by a relative error of at most 0.017.
Values may be sent and summed in bfloat16 or wider, within the bound.
No kernel may reach another device: no remote copies, remote signals or barrier semaphores. Data moves between devices by JAX's collectives and lax.ppermute only.
A program may use at most 64 MiB of HBM per device.

```python
import math
import jax
import jax.numpy as jnp
import numpy as np
from jax import lax

D = 5120
HQ = 40
HK = 8
HD = 128
TOK_DEV = 224
DOCS = 16
TOKENS = 14336
MOST = 7168
N_TP = 8


def draw_queries(key, part):
    key = jax.random.fold_in(key, 11)
    sample = jnp.clip(1.5 * jax.random.normal(key, (TOKENS, HQ * HD), jnp.float32), -8.0, 8.0)
    return sample.astype(jnp.bfloat16)


def draw_keys(key, part):
    key = jax.random.fold_in(key, 23)
    sample = jnp.clip(jax.random.normal(key, (TOKENS, HK * HD), jnp.float32), -8.0, 8.0)
    return sample.astype(jnp.bfloat16)


def block_scale(stream_key, extent, split, least, high):
    loudness, own = 1.0, jax.random.fold_in(stream_key, 6)
    for axis_at, parts in split:
        steps = jnp.exp(jax.random.uniform(jax.random.fold_in(own, axis_at), (parts,), jnp.float32, least / len(split), high / len(split)))
        loudness = loudness * jnp.repeat(steps, extent[axis_at] // parts).reshape([-1 if axis == axis_at else 1 for axis in range(len(extent))])
    return loudness


def profile(amount, total, limit, lean):
    loads = [(1 << 20) // math.isqrt(grade ** lean) + 1 for grade in range(2, amount + 1)]
    rest, counts = total - limit - (amount - 1), [1] * (amount - 1)
    while rest > 0:
        movable = [i for i in range(amount - 1) if counts[i] < limit]
        mass, remaining = sum([loads[i] for i in movable]), rest
        for i in movable:
            more = min(limit - counts[i], max(1, remaining * loads[i] // mass), rest)
            counts[i] = counts[i] + more
            rest = rest - more
    return np.array([limit] + counts)


def uneven_parts(own_key, count, total, bound, slope):
    if count == 2:
        one = jax.random.randint(own_key, (), max(1, total - bound), min(bound, total - 1) + 1)
        return jnp.stack([one, total - one])
    lengths = jnp.asarray(profile(count, total, bound, slope), jnp.int32)
    pairs = (count - 1) // 2
    giver, receiver = lengths[1:1 + 2 * pairs:2], lengths[2:2 + 2 * pairs:2]
    room = jnp.minimum(giver - 1, bound - receiver)
    passed = jax.random.randint(jax.random.fold_in(own_key, 1), (pairs,), 0, 1 << 20) % (room + 1)
    lengths = lengths.at[1:1 + 2 * pairs:2].set(giver - passed).at[2:2 + 2 * pairs:2].set(receiver + passed)
    return lengths[jax.random.permutation(jax.random.fold_in(own_key, 2), count)]


def gaussian(key, dims, scale, most, shards=(), held_as=jnp.bfloat16):
    values = jax.random.normal(key, dims, jnp.float32) * scale
    if len(shards) > 0:
        values = block_scale(key, dims, shards, -0.22, 0.18) * values
    return jnp.clip(values, min=-most, max=most).astype(held_as)


def setup_inputs(seed: int = 0) -> dict:
    seeds = jax.random.split(jax.random.key(seed), 6)
    queries = draw_queries(jax.random.fold_in(seeds[5], 71), 0)
    keys = draw_keys(jax.random.fold_in(seeds[5], 71), 0)
    values = gaussian(seeds[2], (TOKENS, HK * HD), 1.0, 6.0, ((0, 64), (1, 8)))
    doc_lengths = uneven_parts(seeds[3], DOCS, TOKENS, MOST, 2).astype(jnp.int32)
    out_weight = gaussian(seeds[4], (HQ, HD, D), 0.14, 0.83984375, ((0, 8), (1, 64)))
    return {"queries": queries, "keys": keys, "values": values, "doc_lengths": doc_lengths, "out_weight": out_weight}


def document_ids(positions, doc_lengths):
    doc_ends = jnp.cumsum(doc_lengths).astype(jnp.int32)
    return lax.optimization_barrier(jnp.sum((positions[:, None] >= doc_ends[None, :]).astype(jnp.int32), axis=1)).astype(jnp.int32)

def reference(queries, keys, values, doc_lengths, out_weight):
    group_size = HQ // HK
    positions = jnp.arange(TOKENS, dtype=jnp.int32)
    doc_ids = document_ids(positions, doc_lengths)
    padding = jnp.zeros((MOST, HK * HD), keys.dtype)
    keys_padded = jnp.concatenate([padding, keys], axis=0)
    values_padded = jnp.concatenate([padding, values], axis=0)
    docs_padded = jnp.concatenate([jnp.full((MOST,), -1, jnp.int32), doc_ids])
    pos_padded = jnp.concatenate([jnp.full((MOST,), -1, jnp.int32), positions])
    span = MOST + TOK_DEV
    score_scale = 1.0 / math.sqrt(HD)

    def attend(block_index):
        query_start = (block_index * TOK_DEV).astype(jnp.int32)
        query_rows = lax.dynamic_slice_in_dim(queries, query_start, TOK_DEV, 0).astype(jnp.float32)
        query_rows = query_rows.reshape(TOK_DEV, HK, group_size, HD)
        key_rows = lax.dynamic_slice_in_dim(keys_padded, query_start, span, 0).astype(jnp.float32).reshape(span, HK, HD)
        value_rows = lax.dynamic_slice_in_dim(values_padded, query_start, span, 0).astype(jnp.float32).reshape(span, HK, HD)
        key_docs = lax.dynamic_slice_in_dim(docs_padded, query_start, span, 0)
        key_pos = lax.dynamic_slice_in_dim(pos_padded, query_start, span, 0)
        query_docs = lax.dynamic_slice_in_dim(doc_ids, query_start, TOK_DEV, 0)
        query_pos = lax.dynamic_slice_in_dim(positions, query_start, TOK_DEV, 0)
        allowed = (key_pos[None, :] <= query_pos[:, None]) & (key_docs[None, :] == query_docs[:, None])
        scores = jnp.einsum('tkgd,skd->kgts', query_rows, key_rows, precision=lax.Precision.HIGHEST) * score_scale
        masked = jnp.where(allowed, scores, -jnp.inf)
        row_max = lax.optimization_barrier(jnp.max(masked, axis=-1, keepdims=True))
        weights = jnp.where(allowed, jnp.exp(scores - row_max), 0.0)
        totals = lax.optimization_barrier(jnp.sum(weights, axis=-1, keepdims=True))
        rounded = lax.optimization_barrier(weights.astype(jnp.bfloat16)).astype(jnp.float32)
        mixed = jnp.einsum('kgts,skd->kgtd', rounded, value_rows, precision=lax.Precision.HIGHEST) / totals
        mixed = jnp.transpose(mixed, (2, 0, 1, 3)).reshape(TOK_DEV, HQ * HD)
        return mixed.astype(jnp.float32)
    blocks = lax.map(attend, jnp.arange(TOKENS // TOK_DEV, dtype=jnp.int32))
    attended = blocks.reshape(TOKENS, HQ * HD)
    head_groups = HQ // N_TP
    attended_rounded = lax.optimization_barrier(attended.astype(jnp.bfloat16))
    attended_heads = attended_rounded.reshape(TOKENS, HQ, HD).astype(jnp.float32)
    weight_full = out_weight.astype(jnp.float32)
    projected = jnp.zeros((TOKENS, D), jnp.float32)
    for group_index in range(N_TP):
        lower = group_index * head_groups
        upper = lower + head_groups
        partial_value = jnp.einsum('thd,hde->te', attended_heads[:, lower:upper], weight_full[lower:upper], precision=lax.Precision.HIGHEST)
        rounded_part = lax.optimization_barrier(partial_value.astype(jnp.bfloat16))
        projected = projected + rounded_part.astype(jnp.float32)
    return (attended, projected)
```

```python
import functools
import math

import jax
import jax.numpy as jnp
from jax import lax
from jax.experimental import pallas as pl
from jax.experimental.pallas import tpu as pltpu
from jax.sharding import Mesh, PartitionSpec as P

HD = 128
XH, NZ, NC, NY, NX = 2, 16, 2, 4, 2
CHIPS = XH * NZ
ROWS = 224
QROWS = NC * ROWS
HEADS = 5
WIDE = HEADS * HD
STATE = WIDE + 16
FLOOR = -1e29
MASKED = -1e30
NEG = (((1,), (1,)), ((), ()))
RING = ("xh", "z")
VMEM = 40 * 1024 * 1024
F32 = jnp.float32
BF16 = jnp.bfloat16


def attend_kernel(offsets, first, here_ref, len_ref, q_ref, *refs):
    count = len(offsets)
    kv_refs = refs[:count]
    state = refs[-1]
    if first:
        state[:WIDE] = jnp.zeros((WIDE, QROWS), F32)
        state[WIDE : WIDE + 8] = jnp.full((8, QROWS), FLOOR, F32)
        state[WIDE + 8 :] = jnp.zeros((8, QROWS), F32)
    else:
        state[...] = refs[count][...]
    chip, core = here_ref[0], here_ref[1]
    q_start = chip * QROWS
    q_last = q_start + QROWS - 1
    q_pos = q_start + lax.broadcasted_iota(jnp.int32, (1, QROWS), 1)
    doc_start = jnp.zeros((1, QROWS), jnp.int32)
    low, high, end = jnp.int32(0), jnp.int32(0), jnp.int32(0)
    for i in range(len_ref.shape[0]):
        end = end + len_ref[i]
        doc_start = jnp.where(q_pos >= end, end, doc_start)
        low = jnp.where(q_start >= end, end, low)
        high = jnp.where(q_last >= end, end, high)
    scale = math.log2(math.e) / math.sqrt(HD)

    def visit(kv_ref, k_start, partial):
        keys = kv_ref[:ROWS]
        values = kv_ref[ROWS:]
        if partial:
            k_pos = k_start + lax.broadcasted_iota(jnp.int32, (ROWS, QROWS), 0)
            allowed = (k_pos >= doc_start) & (k_pos <= q_pos)
        for h in range(HEADS):
            rows = slice(h * HD, (h + 1) * HD)
            scores = scale * lax.dot_general(keys, q_ref[:, rows], NEG, preferred_element_type=F32)
            if partial:
                scores = jnp.where(allowed, scores, MASKED)
            old = state[WIDE + h : WIDE + h + 1]
            new = jnp.maximum(old, jnp.max(scores, axis=0, keepdims=True))
            fix = jnp.exp2(old - new)
            weights = jnp.exp2(scores - new)
            state[WIDE + h : WIDE + h + 1] = new
            total = slice(WIDE + 8 + h, WIDE + 9 + h)
            state[total] = state[total] * fix + jnp.sum(weights, axis=0, keepdims=True)
            mixed = lax.dot_general(
                values, weights.astype(BF16), (((0,), (0,)), ((), ())), preferred_element_type=F32
            )
            state[rows] = state[rows] * fix + mixed

    for offset, kv_ref in zip(offsets, kv_refs):
        k_start = (chip - offset) * QROWS + core * ROWS
        k_last = k_start + ROWS - 1
        needed = (k_start >= 0) & (k_last >= low) & (k_start <= q_last)
        whole = (k_start >= high) & (k_last <= q_start)
        if offset > 0:
            pl.when(needed & whole)(functools.partial(visit, kv_ref, k_start, False))
        pl.when(needed & jnp.logical_not(whole))(functools.partial(visit, kv_ref, k_start, True))


def attend(here, lengths, q, blocks, state):
    offsets = [offset for offset, _ in blocks]
    operands = [kv for _, kv in blocks]
    smem = pl.BlockSpec(memory_space=pltpu.SMEM)
    vmem = pl.BlockSpec(memory_space=pltpu.VMEM)
    specs = [smem, smem, vmem] + [vmem] * len(operands)
    aliases = {}
    if state is not None:
        aliases = {len(specs): 0}
        operands = operands + [state]
        specs = specs + [vmem]
    pairs = len(offsets) * QROWS * ROWS * HEADS
    return pl.pallas_call(
        functools.partial(attend_kernel, offsets, state is None),
        out_shape=jax.ShapeDtypeStruct((STATE, QROWS), F32),
        in_specs=specs,
        out_specs=vmem,
        input_output_aliases=aliases,
        cost_estimate=pl.CostEstimate(
            flops=pairs * HD * 8, bytes_accessed=STATE * QROWS * 8, transcendentals=pairs
        ),
        compiler_params=pltpu.CompilerParams(vmem_limit_bytes=VMEM),
    )(here, lengths, q, *operands)


def merge_kernel(here_ref, mine_ref, other_ref, out_ref, a_ref, full):
    xh, core = here_ref[2], here_ref[1]
    d = lax.broadcasted_iota(jnp.int32, (HD, HD), 0)
    g = lax.broadcasted_iota(jnp.int32, (HD, HD), 1)
    source = (xh ^ ((g >> 2) & 1)) * (NZ * 4) + (g >> 3) * 4 + (core ^ ((g >> 1) & 1)) * 2 + (g & 1)
    perm = jnp.where(d == source, 1.0, 0.0).astype(BF16)
    for h in range(HEADS):
        rows = slice(h * HD, (h + 1) * HD)
        top = slice(WIDE + h, WIDE + h + 1)
        total = slice(WIDE + 8 + h, WIDE + 9 + h)
        m = jnp.maximum(mine_ref[top], other_ref[top])
        mine, other = jnp.exp2(mine_ref[top] - m), jnp.exp2(other_ref[top] - m)
        den = mine * mine_ref[total] + other * other_ref[total]
        mixed = (mine_ref[rows] * mine + other_ref[rows] * other) / den
        mixed = mixed.T
        full[:, rows] = mixed
        a_ref[:, rows] = jnp.dot(mixed.astype(BF16), perm, preferred_element_type=F32).astype(BF16)
    out_ref[...] = full[pl.ds(pl.multiple_of(core * ROWS, ROWS), ROWS)]


def merge(here, mine, other):
    vmem = pl.BlockSpec(memory_space=pltpu.VMEM)
    return pl.pallas_call(
        merge_kernel,
        out_shape=(
            jax.ShapeDtypeStruct((ROWS, WIDE), F32),
            jax.ShapeDtypeStruct((QROWS, WIDE), BF16),
        ),
        in_specs=[pl.BlockSpec(memory_space=pltpu.SMEM), vmem, vmem],
        out_specs=(vmem, vmem),
        scratch_shapes=[pltpu.VMEM((QROWS, WIDE), F32)],
        cost_estimate=pl.CostEstimate(
            flops=QROWS * WIDE * 300, bytes_accessed=STATE * QROWS * 12, transcendentals=QROWS * 16
        ),
        compiler_params=pltpu.CompilerParams(vmem_limit_bytes=VMEM),
    )(here, mine, other)


def project_kernel(where_ref, a_ref, w_ref, *outs):
    weight = jnp.concatenate([w_ref[:, h * WIDE : (h + 1) * WIDE] for h in range(HEADS)], axis=0)
    for d in range(NC):
        to = where_ref[1] ^ d
        rows = a_ref[pl.ds(pl.multiple_of(to * ROWS, ROWS), ROWS)]
        outs[d][...] = jnp.dot(rows, weight, preferred_element_type=F32).astype(BF16)


def project(where, a, weight):
    whole = pl.BlockSpec((QROWS, WIDE), lambda i, w: (0, 0))
    out = pl.BlockSpec((ROWS, WIDE), lambda i, w: (0, 0))
    return pl.pallas_call(
        project_kernel,
        grid_spec=pltpu.PrefetchScalarGridSpec(
            num_scalar_prefetch=1,
            grid=(1,),
            in_specs=[whole, pl.BlockSpec((HD, HEADS * WIDE), lambda i, w: (0, w[0]))],
            out_specs=[out] * NC,
        ),
        out_shape=[jax.ShapeDtypeStruct((ROWS, WIDE), BF16)] * NC,
        cost_estimate=pl.CostEstimate(
            flops=2 * QROWS * WIDE * WIDE, bytes_accessed=4 * QROWS * WIDE, transcendentals=0
        ),
        compiler_params=pltpu.CompilerParams(vmem_limit_bytes=VMEM),
    )(where, a, weight)


def swap(value, axis):
    return lax.ppermute(value, axis, [(0, 1), (1, 0)])


def ring(value, steps):
    return lax.ppermute(value, RING, [(c, (c + steps) % CHIPS) for c in range(CHIPS)])


def gather_weight(out_weight, core):
    split = out_weight.reshape(HEADS, 2, NY, NX, WIDE)
    halves = [jnp.transpose(split[:, :, :, x], (1, 2, 0, 3)).reshape(2, NY * HEADS * WIDE) for x in range(NX)]
    mine = jnp.where(core == 0, halves[0], halves[1])
    other = jnp.where(core == 0, halves[1], halves[0])
    rows = jnp.concatenate([mine, swap(other, "core")], axis=0)
    rows = jnp.concatenate([rows, swap(rows, "xh")], axis=0)
    return lax.all_gather(rows, "z", axis=0, tiled=True)


def body(queries, keys, values, doc_lengths, out_weight):
    xh, z, core, tp = (lax.axis_index(name) for name in ("xh", "z", "core", "tp"))
    y, xl = tp // NX, tp % NX
    here = jnp.stack([xh * NZ + z, core, xh]).astype(jnp.int32)
    forward = {0: jnp.concatenate([keys, values], axis=0)}
    backward = {0: ring(forward[0], NZ)}
    other_q = swap(queries, "core")
    q = jnp.where(core == 0, jnp.concatenate([queries, other_q]), jnp.concatenate([other_q, queries]))
    weight = gather_weight(out_weight, core)
    for s in range(1, 9):
        forward[s] = ring(forward[s - 1], 1)
        if s < 8:
            backward[s] = ring(backward[s - 1], -1)

    def blocks(*names):
        return [(s, forward[s]) if kind == "f" else (NZ - s, backward[s]) for kind, s in names]

    state = None
    for group in (
        (("f", 0), ("b", 0)),
        (("f", 1), ("b", 1)),
        (("f", 2), ("b", 2), ("f", 3), ("b", 3)),
        (("f", 4), ("b", 4), ("f", 5), ("b", 5)),
        (("f", 6), ("b", 6)),
        (("f", 7), ("b", 7), ("f", 8)),
    ):
        state = attend(here, doc_lengths, q, blocks(*group), state)
    attended, rounded = merge(here, state, swap(state, "core"))
    parts = []
    for dy in (2, 1, 3, 0):
        where = jnp.stack([(y + dy) % NY, xl]).astype(jnp.int32)
        for d, block in enumerate(project(where, rounded, weight)):
            perm = [
                (c * NY * NX + sy * NX + sx, (sx ^ d) * NY * NX + (sy + dy) % NY * NX + c)
                for c in range(NC)
                for sy in range(NY)
                for sx in range(NX)
            ]
            parts.append(lax.ppermute(block, ("core", "tp"), perm))
    projected = functools.reduce(lambda a, b: a + b, [part.astype(F32) for part in parts])
    return (attended, projected)


def solution(mesh):
    fine = Mesh(mesh.devices.reshape(XH, NZ, NC, NY * NX), ("xh", "z", "core", "tp"))
    ctx = ("xh", "z", "core")
    in_specs = (P(ctx, "tp"), P(ctx, "tp"), P(ctx, "tp"), P(), P("tp", ctx, None))
    out_specs = (P(ctx, "tp"), P(ctx, "tp"))
    return jax.shard_map(body, mesh=fine, in_specs=in_specs, out_specs=out_specs, check_vma=False)
```

```python
import functools
import math

import jax
import jax.numpy as jnp
from jax import lax
from jax.experimental import pallas as pl
from jax.experimental.pallas import tpu as pltpu
from jax.sharding import Mesh, PartitionSpec as P

HD = 128
XH, NZ, NC, NY, NX = 2, 16, 2, 4, 2
ROWS = 224
QROWS = NC * ROWS
HEADS = 5
WIDE = HEADS * HD
STATE = WIDE + 16
DEEP = 2 * HD
FLOOR = -1e29
MASKED = -1e30
NEG = (((1,), (1,)), ((), ()))
VMEM = 40 * 1024 * 1024
F32 = jnp.float32
BF16 = jnp.bfloat16


def attend_kernel(visits, first, here_ref, len_ref, q_ref, *refs):
    held, starts, state = refs[-2], refs[-1], refs[-3]
    if first:
        state[:WIDE] = jnp.zeros((WIDE, QROWS), F32)
        state[WIDE : WIDE + 8] = jnp.full((8, QROWS), FLOOR, F32)
        state[WIDE + 8 :] = jnp.zeros((8, QROWS), F32)
    else:
        state[...] = refs[-4][...]
    z, core, xh = here_ref[0], here_ref[1], here_ref[2]
    q_start = (xh * NZ + z) * QROWS
    q_last = q_start + QROWS - 1
    q_pos = q_start + lax.broadcasted_iota(jnp.int32, (1, QROWS), 1)
    doc_start = jnp.zeros((1, QROWS), jnp.int32)
    low, high, end = jnp.int32(0), jnp.int32(0), jnp.int32(0)
    for i in range(len_ref.shape[0]):
        end = end + len_ref[i]
        doc_start = jnp.where(q_pos >= end, end, doc_start)
        low = jnp.where(q_start >= end, end, low)
        high = jnp.where(q_last >= end, end, high)
    scale = math.log2(math.e) / math.sqrt(HD)

    def visit(slot, k_start, partial):
        keys = held[slot, :ROWS]
        values = held[slot, ROWS:].T
        if partial:
            k_pos = k_start + lax.broadcasted_iota(jnp.int32, (ROWS, QROWS), 0)
            allowed = (k_pos >= doc_start) & (k_pos <= q_pos)
        for h in range(HEADS):
            rows = slice(h * HD, (h + 1) * HD)
            scores = scale * lax.dot_general(keys, q_ref[:, rows], NEG, preferred_element_type=F32)
            if partial:
                scores = jnp.where(allowed, scores, MASKED)
            old = state[WIDE + h : WIDE + h + 1]
            new = jnp.maximum(old, jnp.max(scores, axis=0, keepdims=True))
            fix = jnp.exp2(old - new)
            weights = jnp.exp2(scores - new)
            state[WIDE + h : WIDE + h + 1] = new
            total = slice(WIDE + 8 + h, WIDE + 9 + h)
            state[total] = state[total] * fix + jnp.sum(weights, axis=0, keepdims=True)
            mixed = jnp.dot(values, weights.astype(BF16), preferred_element_type=F32)
            state[rows] = state[rows] * fix + mixed

    count = jnp.int32(0)
    for operand, block, offset, other in visits:
        plane = xh ^ 1 if other else xh
        k_start = (plane * NZ + ((z + NZ - offset) & (NZ - 1))) * QROWS + core * ROWS
        needed = (k_start + ROWS > low) & (k_start <= q_last)

        @pl.when(needed)
        def _():
            held[count] = refs[operand][block * QROWS : (block + 1) * QROWS]
            starts[count] = k_start

        count = count + needed.astype(jnp.int32)

    @pl.loop(0, count)
    def _(slot):
        k_start = starts[slot]
        whole = (k_start >= high) & (k_start + ROWS <= q_start + 1)
        pl.when(whole)(functools.partial(visit, slot, k_start, False))
        pl.when(jnp.logical_not(whole))(functools.partial(visit, slot, k_start, True))


def attend(here, lengths, q, visits, operands, state):
    smem = pl.BlockSpec(memory_space=pltpu.SMEM)
    vmem = pl.BlockSpec(memory_space=pltpu.VMEM)
    specs = [smem, smem, vmem] + [vmem] * len(operands)
    aliases = {}
    if state is not None:
        aliases = {len(specs): 0}
        operands = operands + [state]
        specs = specs + [vmem]
    pairs = (len(visits) + 1) // 2 * QROWS * ROWS * HEADS
    return pl.pallas_call(
        functools.partial(attend_kernel, visits, state is None),
        out_shape=jax.ShapeDtypeStruct((STATE, QROWS), F32),
        in_specs=specs,
        out_specs=vmem,
        scratch_shapes=[
            pltpu.VMEM((len(visits), QROWS, HD), BF16),
            pltpu.SMEM((len(visits),), jnp.int32),
        ],
        input_output_aliases=aliases,
        cost_estimate=pl.CostEstimate(
            flops=pairs * HD * 8, bytes_accessed=STATE * QROWS * 8, transcendentals=pairs
        ),
        compiler_params=pltpu.CompilerParams(vmem_limit_bytes=VMEM),
    )(here, lengths, q, *operands)


def merge_kernel(here_ref, mine_ref, other_ref, out_ref, a_ref, full):
    for h in range(HEADS):
        rows = slice(h * HD, (h + 1) * HD)
        top = slice(WIDE + h, WIDE + h + 1)
        total = slice(WIDE + 8 + h, WIDE + 9 + h)
        m = jnp.maximum(mine_ref[top], other_ref[top])
        mine, other = jnp.exp2(mine_ref[top] - m), jnp.exp2(other_ref[top] - m)
        den = mine * mine_ref[total] + other * other_ref[total]
        mixed = (mine_ref[rows] * mine + other_ref[rows] * other) / den
        full[:, rows] = mixed.T
    own = full[pl.ds(pl.multiple_of(here_ref[1] * ROWS, ROWS), ROWS)]
    out_ref[...] = own
    a_ref[...] = own.astype(BF16)


def merge(here, mine, other):
    vmem = pl.BlockSpec(memory_space=pltpu.VMEM)
    return pl.pallas_call(
        merge_kernel,
        out_shape=(
            jax.ShapeDtypeStruct((ROWS, WIDE), F32),
            jax.ShapeDtypeStruct((ROWS, WIDE), BF16),
        ),
        in_specs=[pl.BlockSpec(memory_space=pltpu.SMEM), vmem, vmem],
        out_specs=(vmem, vmem),
        scratch_shapes=[pltpu.VMEM((QROWS, WIDE), F32)],
        cost_estimate=pl.CostEstimate(
            flops=QROWS * WIDE * 100, bytes_accessed=STATE * QROWS * 12, transcendentals=QROWS * 16
        ),
        compiler_params=pltpu.CompilerParams(vmem_limit_bytes=VMEM),
    )(here, mine, other)


def project_kernel(first, here_ref, near_ref, far_ref, own_ref, other_ref, *refs):
    core, xh, xl = here_ref[2], here_ref[3], here_ref[4]
    k = lax.broadcasted_iota(jnp.int32, (DEEP, DEEP), 0)
    g = lax.broadcasted_iota(jnp.int32, (DEEP, DEEP), 1)
    source_core = core ^ (g >> 7)
    row = g & (HD - 1)
    d = (xh ^ ((row >> 1) & 1)) * (NZ * 4) + (row >> 3) * 4 + source_core * 2 + (row & 1)
    source_x = xl ^ (k >> 7)
    match = ((k & (HD - 1)) == d) & (((row >> 2) & 1) == source_x)
    perm = jnp.where(match, 1.0, 0.0).astype(BF16)
    total = jnp.zeros((ROWS, WIDE), F32) if first else refs[0][...]
    for h in range(HEADS):
        heads = slice(h * HD, (h + 1) * HD)
        columns = slice(h * WIDE, (h + 1) * WIDE)
        both = jnp.concatenate([near_ref[:, heads], far_ref[:, heads]], axis=1)
        moved = jnp.dot(both, perm, preferred_element_type=F32).astype(BF16)
        weight = jnp.concatenate([own_ref[:, columns], other_ref[:, columns]], axis=0)
        total += jnp.dot(moved, weight, preferred_element_type=F32)
    refs[-1][...] = total


def project(where, near, far, weights, total):
    block = pl.BlockSpec((ROWS, WIDE), lambda i, w: (0, 0))
    weight = pl.BlockSpec((HD, HEADS * WIDE), lambda i, w: (0, w[0]))
    totals = [] if total is None else [total]
    return pl.pallas_call(
        functools.partial(project_kernel, total is None),
        grid_spec=pltpu.PrefetchScalarGridSpec(
            num_scalar_prefetch=1,
            grid=(1,),
            in_specs=[block, block, weight, weight] + [block] * len(totals),
            out_specs=block,
        ),
        out_shape=jax.ShapeDtypeStruct((ROWS, WIDE), F32),
        cost_estimate=pl.CostEstimate(
            flops=2 * ROWS * DEEP * HEADS * (WIDE + DEEP),
            bytes_accessed=DEEP * HEADS * WIDE * 2,
            transcendentals=0,
        ),
        compiler_params=pltpu.CompilerParams(vmem_limit_bytes=VMEM),
    )(where, near, far, *weights, *totals)


def swap(value, axis):
    return lax.ppermute(value, axis, [(0, 1), (1, 0)])


def ring(value, steps):
    return lax.ppermute(value, "z", [(i, (i + steps) % NZ) for i in range(NZ)])


def hop(block, dy, dx):
    perm = [
        (sy * NX + sx, (sy + dy) % NY * NX + (sx ^ dx)) for sy in range(NY) for sx in range(NX)
    ]
    return lax.ppermute(block, "tp", perm)


def split_kernel(after_ref, weight_ref, out_ref):
    for j in range(NY * NX):
        for h in range(HEADS):
            out_ref[j, :, h * WIDE : (h + 1) * WIDE] = weight_ref[h, :, j * WIDE : (j + 1) * WIDE]


def stack_kernel(mine_ref, other_ref, out_ref):
    for e in range(NX):
        for rel, ref in enumerate((mine_ref, other_ref)):
            row = e * 4 + rel * 2
            for y in range(NY):
                lanes = slice(y * HEADS * WIDE, (y + 1) * HEADS * WIDE)
                out_ref[row : row + 2, lanes] = ref[y * NX + e]


def pass_kernel(across_ref, below_ref, weight_ref, out_ref):
    pass


def gather_weight(out_weight, after):
    whole = pl.BlockSpec(memory_space=pl.ANY)
    vmem = pl.BlockSpec(memory_space=pltpu.VMEM)
    split = pl.pallas_call(
        split_kernel,
        out_shape=jax.ShapeDtypeStruct((NY * NX, 2, HEADS * WIDE), BF16),
        in_specs=[whole, vmem],
        out_specs=vmem,
    )(after, out_weight)
    split = lax.all_to_all(split, "tp", 0, 0)
    rows = pl.pallas_call(
        stack_kernel,
        out_shape=jax.ShapeDtypeStruct((8, NY * HEADS * WIDE), BF16),
        in_specs=[vmem, vmem],
        out_specs=vmem,
    )(split, swap(split, "xh"))
    return lax.all_gather(rows, "z", axis=0, tiled=True)


def exchange_weight(own, across, below):
    whole = pl.BlockSpec(memory_space=pl.ANY)
    hbm = pl.BlockSpec(memory_space=pltpu.HBM)
    own = pl.pallas_call(
        pass_kernel,
        out_shape=jax.ShapeDtypeStruct(own.shape, own.dtype),
        in_specs=[whole, whole, hbm],
        out_specs=hbm,
        input_output_aliases={2: 0},
    )(across, below, own)
    return own, swap(own, "core")


def body(queries, keys, values, doc_lengths, out_weight):
    xh, z, core, tp = (lax.axis_index(name) for name in ("xh", "z", "core", "tp"))
    y, xl = tp // NX, tp % NX
    here = jnp.stack([z, core, xh, xl]).astype(jnp.int32)
    own = jnp.concatenate([keys, values], axis=0)
    pair = jnp.concatenate([own, swap(own, "xh")], axis=0)
    weight = gather_weight(out_weight, pair)
    other_q = swap(queries, "core")
    q = jnp.where(core == 0, jnp.concatenate([queries, other_q]), jnp.concatenate([other_q, queries]))
    up, down = {0: pair}, {0: pair}
    for s in range(1, NZ // 2):
        up[s] = ring(up[s - 1], 1)
        down[s] = ring(down[s - 1], -1)
    far = NZ // 2
    last_up = ring(up[far - 1][:QROWS], 1)
    last_down = ring(down[far - 1][QROWS:], -1)

    state = attend(here, doc_lengths, q, [(0, 0, 0, False), (0, 1, 0, True)], [pair], None)
    for steps in ((1,), (2, 3), (4, 5), (6,), (7,)):
        visits, operands = [], []
        for s in steps:
            for offset, block in ((s, up[s]), (-s, down[s])):
                visits += [(len(operands), 0, offset, False), (len(operands), 1, offset, True)]
                operands.append(block)
        state = attend(here, doc_lengths, q, visits, operands, state)
    visits = [(0, 0, far, False), (1, 0, far, True)]
    state = attend(here, doc_lengths, q, visits, [last_up, last_down], state)
    attended, a = merge(here, state, swap(state, "core"))

    across = hop(a, 0, 1)
    below, above = hop(a, 1, 0), hop(a, -1, 0)
    weights = exchange_weight(weight, across, below)
    two = hop(below, 1, 0)
    across_below, across_above = hop(across, 1, 0), hop(across, -1, 0)
    across_two = hop(across_above, -1, 0)
    projected = None
    for dy, near, far in (
        (0, a, across),
        (-1, below, across_below),
        (1, above, across_above),
        (2, two, across_two),
    ):
        where = jnp.stack([(y + dy + NY) % NY, z, core, xh, xl]).astype(jnp.int32)
        projected = project(where, near, far, weights, projected)
    return (attended, projected)


def solution(mesh):
    fine = Mesh(mesh.devices.reshape(XH, NZ, NC, NY * NX), ("xh", "z", "core", "tp"))
    ctx = ("xh", "z", "core")
    in_specs = (P(ctx, "tp"), P(ctx, "tp"), P(ctx, "tp"), P(), P("tp", ctx, None))
    out_specs = (P(ctx, "tp"), P(ctx, "tp"))
    return jax.shard_map(body, mesh=fine, in_specs=in_specs, out_specs=out_specs, check_vma=False)
```

```python
import functools
import math

import jax
import jax.numpy as jnp
from jax import lax
from jax.experimental import pallas as pl
from jax.experimental.pallas import tpu as pltpu
from jax.sharding import Mesh, PartitionSpec as P

HD = 128
XH, NZ, NC, NY, NX = 2, 16, 2, 4, 2
ROWS = 224
QROWS = NC * ROWS
HEADS = 5
WIDE = HEADS * HD
STATE = WIDE + 16
DEEP = 2 * HD
COST = 64
FLOOR = -1e29
MASKED = -1e30
NEG = (((1,), (1,)), ((), ()))
VMEM = 40 * 1024 * 1024
F32 = jnp.float32
BF16 = jnp.bfloat16


def attend_kernel(visits, first, here_ref, len_ref, q_ref, *refs):
    held, starts, state = refs[-2], refs[-1], refs[-3]
    if first:
        state[:WIDE] = jnp.zeros((WIDE, QROWS), F32)
        state[WIDE : WIDE + 8] = jnp.full((8, QROWS), FLOOR, F32)
        state[WIDE + 8 :] = jnp.zeros((8, QROWS), F32)
    else:
        state[...] = refs[-4][...]
    z, core, xh = here_ref[0], here_ref[1], here_ref[2]
    q_start = (xh * NZ + z) * QROWS
    q_last = q_start + QROWS - 1
    q_pos = q_start + lax.broadcasted_iota(jnp.int32, (1, QROWS), 1)
    doc_start = jnp.zeros((1, QROWS), jnp.int32)
    low, high, end = jnp.int32(0), jnp.int32(0), jnp.int32(0)
    for i in range(len_ref.shape[0]):
        end = end + len_ref[i]
        doc_start = jnp.where(q_pos >= end, end, doc_start)
        low = jnp.where(q_start >= end, end, low)
        high = jnp.where(q_last >= end, end, high)
    scale = math.log2(math.e) / math.sqrt(HD)

    def visit(slot, k_start, partial):
        keys = held[slot, :ROWS]
        values = held[slot, ROWS:].T
        if partial:
            k_pos = k_start + lax.broadcasted_iota(jnp.int32, (ROWS, QROWS), 0)
            allowed = (k_pos >= doc_start) & (k_pos <= q_pos)
        for h in range(HEADS):
            rows = slice(h * HD, (h + 1) * HD)
            scores = scale * lax.dot_general(keys, q_ref[:, rows], NEG, preferred_element_type=F32)
            if partial:
                scores = jnp.where(allowed, scores, MASKED)
            old = state[WIDE + h : WIDE + h + 1]
            new = jnp.maximum(old, jnp.max(scores, axis=0, keepdims=True))
            fix = jnp.exp2(old - new)
            weights = jnp.exp2(scores - new)
            state[WIDE + h : WIDE + h + 1] = new
            total = slice(WIDE + 8 + h, WIDE + 9 + h)
            state[total] = state[total] * fix + jnp.sum(weights, axis=0, keepdims=True)
            mixed = jnp.dot(values, weights.astype(BF16), preferred_element_type=F32)
            state[rows] = state[rows] * fix + mixed

    count = jnp.int32(0)
    for operand, block, offset, other in visits:
        plane = xh ^ 1 if other else xh
        k_start = (plane * NZ + ((z + NZ - offset) & (NZ - 1))) * QROWS + core * ROWS
        needed = (k_start + ROWS > low) & (k_start <= q_last)

        @pl.when(needed)
        def _():
            held[count] = refs[operand][block * QROWS : (block + 1) * QROWS]
            starts[count] = k_start

        count = count + needed.astype(jnp.int32)

    @pl.loop(0, count)
    def _(slot):
        k_start = starts[slot]
        whole = (k_start >= high) & (k_start + ROWS <= q_start + 1)
        pl.when(whole)(functools.partial(visit, slot, k_start, False))
        pl.when(jnp.logical_not(whole))(functools.partial(visit, slot, k_start, True))


def attend(here, lengths, q, visits, operands, state):
    smem = pl.BlockSpec(memory_space=pltpu.SMEM)
    vmem = pl.BlockSpec(memory_space=pltpu.VMEM)
    specs = [smem, smem, vmem] + [vmem] * len(operands)
    aliases = {}
    if state is not None:
        aliases = {len(specs): 0}
        operands = operands + [state]
        specs = specs + [vmem]
    pairs = (len(visits) + 1) // 2 * QROWS * ROWS * HEADS
    return pl.pallas_call(
        functools.partial(attend_kernel, visits, state is None),
        out_shape=jax.ShapeDtypeStruct((STATE, QROWS), F32),
        in_specs=specs,
        out_specs=vmem,
        scratch_shapes=[
            pltpu.VMEM((len(visits), QROWS, HD), BF16),
            pltpu.SMEM((len(visits),), jnp.int32),
        ],
        input_output_aliases=aliases,
        cost_estimate=pl.CostEstimate(
            flops=pairs * HD * COST, bytes_accessed=STATE * QROWS * COST, transcendentals=pairs
        ),
        compiler_params=pltpu.CompilerParams(vmem_limit_bytes=VMEM),
    )(here, lengths, q, *operands)


def merge_kernel(here_ref, mine_ref, other_ref, out_ref, a_ref, full):
    for h in range(HEADS):
        rows = slice(h * HD, (h + 1) * HD)
        top = slice(WIDE + h, WIDE + h + 1)
        total = slice(WIDE + 8 + h, WIDE + 9 + h)
        m = jnp.maximum(mine_ref[top], other_ref[top])
        mine, other = jnp.exp2(mine_ref[top] - m), jnp.exp2(other_ref[top] - m)
        den = mine * mine_ref[total] + other * other_ref[total]
        mixed = (mine_ref[rows] * mine + other_ref[rows] * other) / den
        full[:, rows] = mixed.T
    own = full[pl.ds(pl.multiple_of(here_ref[1] * ROWS, ROWS), ROWS)]
    out_ref[...] = own
    a_ref[...] = own.astype(BF16)


def merge(here, mine, other):
    vmem = pl.BlockSpec(memory_space=pltpu.VMEM)
    return pl.pallas_call(
        merge_kernel,
        out_shape=(
            jax.ShapeDtypeStruct((ROWS, WIDE), F32),
            jax.ShapeDtypeStruct((ROWS, WIDE), BF16),
        ),
        in_specs=[pl.BlockSpec(memory_space=pltpu.SMEM), vmem, vmem],
        out_specs=(vmem, vmem),
        scratch_shapes=[pltpu.VMEM((QROWS, WIDE), F32)],
        cost_estimate=pl.CostEstimate(
            flops=QROWS * WIDE * 100, bytes_accessed=STATE * QROWS * 12, transcendentals=QROWS * 16
        ),
        compiler_params=pltpu.CompilerParams(vmem_limit_bytes=VMEM),
    )(here, mine, other)


def project_kernel(steps, here_ref, own_ref, other_ref, *refs):
    z, core, xh, xl, y = (here_ref[i] for i in range(5))
    k = lax.broadcasted_iota(jnp.int32, (DEEP, DEEP), 0)
    g = lax.broadcasted_iota(jnp.int32, (DEEP, DEEP), 1)
    row = g & (HD - 1)
    d = (xh ^ ((row >> 1) & 1)) * (NZ * 4) + (row >> 3) * 4 + (core ^ (g >> 7)) * 2 + (row & 1)
    match = ((k & (HD - 1)) == d) & (((row >> 2) & 1) == (xl ^ (k >> 7)))
    perm = jnp.where(match, 1.0, 0.0).astype(BF16)
    near_refs, far_refs = refs[: len(steps)], refs[len(steps) : 2 * len(steps)]
    total = jnp.zeros((ROWS, WIDE), F32) if len(refs) == 2 * len(steps) + 1 else refs[-2][...]
    for step, near_ref, far_ref in zip(steps, near_refs, far_refs):
        start = ((y + step + NY) & (NY - 1)) * (HEADS * WIDE)
        for h in range(HEADS):
            heads = slice(h * HD, (h + 1) * HD)
            columns = pl.ds(pl.multiple_of(start + h * WIDE, HD), WIDE)
            both = jnp.concatenate([near_ref[:, heads], far_ref[:, heads]], axis=1)
            moved = jnp.dot(both, perm, preferred_element_type=F32).astype(BF16)
            weight = jnp.concatenate([own_ref[:, columns], other_ref[:, columns]], axis=0)
            total += jnp.dot(moved, weight, preferred_element_type=F32)
    refs[-1][...] = total


def project(here, weights, pairs, total):
    steps = [step for step, _, _ in pairs]
    operands = [near for _, near, _ in pairs] + [far for _, _, far in pairs]
    operands += [] if total is None else [total]
    vmem = pl.BlockSpec(memory_space=pltpu.VMEM)
    return pl.pallas_call(
        functools.partial(project_kernel, steps),
        out_shape=jax.ShapeDtypeStruct((ROWS, WIDE), F32),
        in_specs=[pl.BlockSpec(memory_space=pltpu.SMEM)] + [vmem] * (2 + len(operands)),
        out_specs=vmem,
        cost_estimate=pl.CostEstimate(
            flops=2 * len(steps) * ROWS * DEEP * HEADS * (WIDE + DEEP),
            bytes_accessed=DEEP * NY * HEADS * WIDE * 2,
            transcendentals=0,
        ),
        compiler_params=pltpu.CompilerParams(vmem_limit_bytes=VMEM),
    )(here, *weights, *operands)


def swap(value, axis):
    return lax.ppermute(value, axis, [(0, 1), (1, 0)])


def ring(value, steps):
    return lax.ppermute(value, "z", [(i, (i + steps) % NZ) for i in range(NZ)])


def hop(block, dy, dx):
    perm = [
        (sy * NX + sx, (sy + dy) % NY * NX + (sx ^ dx)) for sy in range(NY) for sx in range(NX)
    ]
    return lax.ppermute(block, "tp", perm)


def split_kernel(after_ref, weight_ref, out_ref):
    for j in range(NY * NX):
        for h in range(HEADS):
            out_ref[j, :, h * WIDE : (h + 1) * WIDE] = weight_ref[h, :, j * WIDE : (j + 1) * WIDE]


def stack_kernel(mine_ref, other_ref, out_ref):
    for e in range(NX):
        for rel, ref in enumerate((mine_ref, other_ref)):
            row = e * 4 + rel * 2
            for y in range(NY):
                lanes = slice(y * HEADS * WIDE, (y + 1) * HEADS * WIDE)
                out_ref[row : row + 2, lanes] = ref[y * NX + e]


def pass_kernel(*refs):
    pass


def gather_weight(out_weight, after):
    whole = pl.BlockSpec(memory_space=pl.ANY)
    vmem = pl.BlockSpec(memory_space=pltpu.VMEM)
    split = pl.pallas_call(
        split_kernel,
        out_shape=jax.ShapeDtypeStruct((NY * NX, 2, HEADS * WIDE), BF16),
        in_specs=[whole, vmem],
        out_specs=vmem,
    )(after, out_weight)
    split = lax.all_to_all(split, "tp", 0, 0)
    rows = pl.pallas_call(
        stack_kernel,
        out_shape=jax.ShapeDtypeStruct((8, NY * HEADS * WIDE), BF16),
        in_specs=[vmem, vmem],
        out_specs=vmem,
    )(split, swap(split, "xh"))
    return lax.all_gather(rows, "z", axis=0, tiled=True)


def exchange_weight(own, *after):
    whole = pl.BlockSpec(memory_space=pl.ANY)
    hbm = pl.BlockSpec(memory_space=pltpu.HBM)
    own = pl.pallas_call(
        pass_kernel,
        out_shape=jax.ShapeDtypeStruct(own.shape, own.dtype),
        in_specs=[whole] * len(after) + [hbm],
        out_specs=hbm,
        input_output_aliases={len(after): 0},
    )(*after, own)
    return own, swap(own, "core")


def body(queries, keys, values, doc_lengths, out_weight):
    xh, z, core, tp = (lax.axis_index(name) for name in ("xh", "z", "core", "tp"))
    here = jnp.stack([z, core, xh, tp % NX, tp // NX]).astype(jnp.int32)
    own = jnp.concatenate([keys, values], axis=0)
    pair = jnp.concatenate([own, swap(own, "xh")], axis=0)
    other_q = swap(queries, "core")
    q = jnp.where(core == 0, jnp.concatenate([queries, other_q]), jnp.concatenate([other_q, queries]))
    up, down = [pair], [pair]
    far = NZ // 2
    for _ in range(1, far):
        up.append(ring(up[-1], 1))
        down.append(ring(down[-1], -1))
    last = [ring(up[-1][:QROWS], 1), ring(down[-1][QROWS:], -1)]
    weight = gather_weight(out_weight, up[1])

    state = attend(here, doc_lengths, q, [(0, 0, 0, False), (0, 1, 0, True)], [pair], None)
    for s in range(1, far):
        visits = [(0, 0, s, False), (0, 1, s, True), (1, 0, -s, False), (1, 1, -s, True)]
        state = attend(here, doc_lengths, q, visits, [up[s], down[s]], state)
    state = attend(here, doc_lengths, q, [(0, 0, far, False), (1, 0, far, True)], last, state)
    attended, a = merge(here, state, swap(state, "core"))

    below, above = hop(a, 1, 0), hop(a, -1, 0)
    across_below, across_above, across = hop(a, 1, 1), hop(a, -1, 1), hop(a, 0, 1)
    two, across_two = hop(below, 1, 0), hop(across_above, -1, 0)
    weights = exchange_weight(weight, below, above, across_below, across_above, across)
    pairs = [(0, a, across), (-1, below, across_below), (1, above, across_above)]
    projected = project(here, weights, pairs, None)
    projected = project(here, weights, [(2, two, across_two)], projected)
    return (attended, projected)


def solution(mesh):
    fine = Mesh(mesh.devices.reshape(XH, NZ, NC, NY * NX), ("xh", "z", "core", "tp"))
    ctx = ("xh", "z", "core")
    in_specs = (P(ctx, "tp"), P(ctx, "tp"), P(ctx, "tp"), P(), P("tp", ctx, None))
    out_specs = (P(ctx, "tp"), P(ctx, "tp"))
    return jax.shard_map(body, mesh=fine, in_specs=in_specs, out_specs=out_specs, check_vma=False)
```

```python
import functools
import math

import jax
import jax.numpy as jnp
from jax import lax
from jax.experimental import pallas as pl
from jax.experimental.pallas import tpu as pltpu
from jax.sharding import Mesh, PartitionSpec as P

HD = 128
XH, NZ, NC, NY, NX = 2, 16, 2, 4, 2
ROWS = 224
QROWS = NC * ROWS
HEADS = 5
WIDE = HEADS * HD
STATE = WIDE + 16
DEEP = 2 * HD
FLOOR = -1e29
MASKED = -1e30
NEG = (((1,), (1,)), ((), ()))
VMEM = 40 * 1024 * 1024
F32 = jnp.float32
BF16 = jnp.bfloat16


def attend_kernel(here_ref, len_ref, q_ref, own_ref, far_ref, state):
    state[:WIDE] = jnp.zeros((WIDE, QROWS), F32)
    state[WIDE : WIDE + 8] = jnp.full((8, QROWS), FLOOR, F32)
    state[WIDE + 8 :] = jnp.zeros((8, QROWS), F32)
    z, core, xh = here_ref[0], here_ref[1], here_ref[2]
    q_start = (xh * NZ + z) * QROWS
    q_last = q_start + QROWS - 1
    q_pos = q_start + lax.broadcasted_iota(jnp.int32, (1, QROWS), 1)
    doc_start = jnp.zeros((1, QROWS), jnp.int32)
    low, high, end = jnp.int32(0), jnp.int32(0), jnp.int32(0)
    for i in range(len_ref.shape[0]):
        end = end + len_ref[i]
        doc_start = jnp.where(q_pos >= end, end, doc_start)
        low = jnp.where(q_start >= end, end, low)
        high = jnp.where(q_last >= end, end, high)
    scale = math.log2(math.e) / math.sqrt(HD)

    def visit(keys, values, k_start, partial):
        values = values.T
        if partial:
            k_pos = k_start + lax.broadcasted_iota(jnp.int32, (ROWS, QROWS), 0)
            allowed = (k_pos >= doc_start) & (k_pos <= q_pos)
        for h in range(HEADS):
            rows = slice(h * HD, (h + 1) * HD)
            scores = scale * lax.dot_general(keys, q_ref[:, rows], NEG, preferred_element_type=F32)
            if partial:
                scores = jnp.where(allowed, scores, MASKED)
            old = state[WIDE + h : WIDE + h + 1]
            new = jnp.maximum(old, jnp.max(scores, axis=0, keepdims=True))
            fix = jnp.exp2(old - new)
            weights = jnp.exp2(scores - new)
            state[WIDE + h : WIDE + h + 1] = new
            total = slice(WIDE + 8 + h, WIDE + 9 + h)
            state[total] = state[total] * fix + jnp.sum(weights, axis=0, keepdims=True)
            mixed = jnp.dot(values, weights.astype(BF16), preferred_element_type=F32)
            state[rows] = state[rows] * fix + mixed

    visit(own_ref[:ROWS], own_ref[ROWS:], q_start + core * ROWS, True)

    @pl.loop(0, NZ)
    def _(source):
        plane = jnp.where(source < z, xh, xh ^ 1)
        k_start = (plane * NZ + source) * QROWS + core * ROWS
        needed = (k_start + ROWS > low) & (k_start <= q_last)
        whole = (k_start >= high) & (k_start + ROWS <= q_start + 1)

        def far(partial):
            visit(far_ref[source, :ROWS], far_ref[source, ROWS:], k_start, partial)

        pl.when(needed & whole)(functools.partial(far, False))
        pl.when(needed & jnp.logical_not(whole))(functools.partial(far, True))


def attend(here, lengths, q, own, far):
    smem = pl.BlockSpec(memory_space=pltpu.SMEM)
    vmem = pl.BlockSpec(memory_space=pltpu.VMEM)
    pairs = NZ * QROWS * ROWS * HEADS
    return pl.pallas_call(
        attend_kernel,
        out_shape=jax.ShapeDtypeStruct((STATE, QROWS), F32),
        in_specs=[smem, smem, vmem, vmem, vmem],
        out_specs=vmem,
        cost_estimate=pl.CostEstimate(
            flops=pairs * HD * 4, bytes_accessed=STATE * QROWS * 8, transcendentals=pairs
        ),
        compiler_params=pltpu.CompilerParams(vmem_limit_bytes=VMEM),
    )(here, lengths, q, own, far)


def merge_kernel(here_ref, mine_ref, other_ref, out_ref, a_ref, full):
    for h in range(HEADS):
        rows = slice(h * HD, (h + 1) * HD)
        top = slice(WIDE + h, WIDE + h + 1)
        total = slice(WIDE + 8 + h, WIDE + 9 + h)
        m = jnp.maximum(mine_ref[top], other_ref[top])
        mine, other = jnp.exp2(mine_ref[top] - m), jnp.exp2(other_ref[top] - m)
        den = mine * mine_ref[total] + other * other_ref[total]
        mixed = (mine_ref[rows] * mine + other_ref[rows] * other) / den
        full[:, rows] = mixed.T
    own = full[pl.ds(pl.multiple_of(here_ref[1] * ROWS, ROWS), ROWS)]
    out_ref[...] = own
    a_ref[...] = own.astype(BF16)


def merge(here, mine, other):
    vmem = pl.BlockSpec(memory_space=pltpu.VMEM)
    return pl.pallas_call(
        merge_kernel,
        out_shape=(
            jax.ShapeDtypeStruct((ROWS, WIDE), F32),
            jax.ShapeDtypeStruct((ROWS, WIDE), BF16),
        ),
        in_specs=[pl.BlockSpec(memory_space=pltpu.SMEM), vmem, vmem],
        out_specs=(vmem, vmem),
        scratch_shapes=[pltpu.VMEM((QROWS, WIDE), F32)],
        cost_estimate=pl.CostEstimate(
            flops=QROWS * WIDE * 100, bytes_accessed=STATE * QROWS * 12, transcendentals=QROWS * 16
        ),
        compiler_params=pltpu.CompilerParams(vmem_limit_bytes=VMEM),
    )(here, mine, other)


def project_kernel(here_ref, own_ref, other_ref, a_ref, out_ref):
    core, xh = here_ref[1], here_ref[2]
    k = lax.broadcasted_iota(jnp.int32, (DEEP, DEEP), 0)
    g = lax.broadcasted_iota(jnp.int32, (DEEP, DEEP), 1)
    row = g & (HD - 1)
    d = (xh ^ ((row >> 1) & 1)) * (NZ * 4) + (row >> 3) * 4 + (core ^ (g >> 7)) * 2 + (row & 1)
    match = ((k & (HD - 1)) == d) & (((row >> 2) & 1) == (k >> 7))
    perm = jnp.where(match, 1.0, 0.0).astype(BF16)
    total = jnp.zeros((ROWS, WIDE), F32)
    for y in range(NY):
        for h in range(HEADS):
            heads = slice(h * HD, (h + 1) * HD)
            columns = slice((y * HEADS + h) * WIDE, (y * HEADS + h + 1) * WIDE)
            both = jnp.concatenate([a_ref[y * NX + x, :, heads] for x in range(NX)], axis=1)
            moved = jnp.dot(both, perm, preferred_element_type=F32).astype(BF16)
            weight = jnp.concatenate([own_ref[:, columns], other_ref[:, columns]], axis=0)
            total += jnp.dot(moved, weight, preferred_element_type=F32)
    out_ref[...] = total


def project(here, weights, a):
    vmem = pl.BlockSpec(memory_space=pltpu.VMEM)
    return pl.pallas_call(
        project_kernel,
        out_shape=jax.ShapeDtypeStruct((ROWS, WIDE), F32),
        in_specs=[pl.BlockSpec(memory_space=pltpu.SMEM), vmem, vmem, vmem],
        out_specs=vmem,
        cost_estimate=pl.CostEstimate(
            flops=2 * NY * ROWS * DEEP * HEADS * (WIDE + DEEP),
            bytes_accessed=DEEP * NY * HEADS * WIDE * 2,
            transcendentals=0,
        ),
        compiler_params=pltpu.CompilerParams(vmem_limit_bytes=VMEM),
    )(here, *weights, a)


def swap(value, axis):
    return lax.ppermute(value, axis, [(0, 1), (1, 0)])


def split_kernel(after_ref, weight_ref, out_ref):
    for j in range(NY * NX):
        for h in range(HEADS):
            out_ref[j, :, h * WIDE : (h + 1) * WIDE] = weight_ref[h, :, j * WIDE : (j + 1) * WIDE]


def stack_kernel(mine_ref, other_ref, out_ref):
    for e in range(NX):
        for rel, ref in enumerate((mine_ref, other_ref)):
            row = e * 4 + rel * 2
            for y in range(NY):
                lanes = slice(y * HEADS * WIDE, (y + 1) * HEADS * WIDE)
                out_ref[row : row + 2, lanes] = ref[y * NX + e]


def pass_kernel(*refs):
    pass


def gather_weight(out_weight, after):
    whole = pl.BlockSpec(memory_space=pl.ANY)
    vmem = pl.BlockSpec(memory_space=pltpu.VMEM)
    split = pl.pallas_call(
        split_kernel,
        out_shape=jax.ShapeDtypeStruct((NY * NX, 2, HEADS * WIDE), BF16),
        in_specs=[whole, vmem],
        out_specs=vmem,
    )(after, out_weight)
    split = lax.all_to_all(split, "tp", 0, 0)
    rows = pl.pallas_call(
        stack_kernel,
        out_shape=jax.ShapeDtypeStruct((8, NY * HEADS * WIDE), BF16),
        in_specs=[vmem, vmem],
        out_specs=vmem,
    )(split, swap(split, "xh"))
    return lax.all_gather(rows, "z", axis=0, tiled=True)


def exchange_weight(own, *after):
    whole = pl.BlockSpec(memory_space=pl.ANY)
    hbm = pl.BlockSpec(memory_space=pltpu.HBM)
    own = pl.pallas_call(
        pass_kernel,
        out_shape=jax.ShapeDtypeStruct(own.shape, own.dtype),
        in_specs=[whole] * len(after) + [hbm],
        out_specs=hbm,
        input_output_aliases={len(after): 0},
    )(*after, own)
    return own, swap(own, "core")


def body(queries, keys, values, doc_lengths, out_weight):
    xh, z, core = (lax.axis_index(name) for name in ("xh", "z", "core"))
    here = jnp.stack([z, core, xh]).astype(jnp.int32)
    own = jnp.concatenate([keys, values], axis=0)
    other = swap(own, "xh")
    above = jnp.arange(NZ, dtype=jnp.int32)[:, None, None] > z
    blocks = jnp.where(above, own[None], other[None])
    far = lax.all_to_all(blocks, "z", 0, 0)
    weight = gather_weight(out_weight, blocks)
    other_q = swap(queries, "core")
    q = jnp.where(core == 0, jnp.concatenate([queries, other_q]), jnp.concatenate([other_q, queries]))
    state = attend(here, doc_lengths, q, own, far)
    attended, a = merge(here, state, swap(state, "core"))
    sources = lax.all_to_all(jnp.broadcast_to(a[None], (NY * NX, ROWS, WIDE)), "tp", 0, 0)
    projected = project(here, exchange_weight(weight, a), sources)
    return (attended, projected)


def solution(mesh):
    fine = Mesh(mesh.devices.reshape(XH, NZ, NC, NY * NX), ("xh", "z", "core", "tp"))
    ctx = ("xh", "z", "core")
    in_specs = (P(ctx, "tp"), P(ctx, "tp"), P(ctx, "tp"), P(), P("tp", ctx, None))
    out_specs = (P(ctx, "tp"), P(ctx, "tp"))
    return jax.shard_map(body, mesh=fine, in_specs=in_specs, out_specs=out_specs, check_vma=False)
```

```python
import functools
import math

import jax
import jax.numpy as jnp
from jax import lax
from jax.experimental import pallas as pl
from jax.experimental.pallas import tpu as pltpu
from jax.sharding import Mesh, PartitionSpec as P

HD = 128
XH, NZ, NC, NY, NX = 2, 16, 2, 4, 2
ROWS = 224
QROWS = NC * ROWS
HEADS = 5
WIDE = HEADS * HD
STATE = WIDE + 16
DEEP = 2 * HD
COST = 64
FLOOR = -1e29
MASKED = -1e30
NEG = (((1,), (1,)), ((), ()))
VMEM = 40 * 1024 * 1024
F32 = jnp.float32
BF16 = jnp.bfloat16


def attend_kernel(visits, first, here_ref, len_ref, q_ref, *refs):
    held, starts, state = refs[-2], refs[-1], refs[-3]
    if first:
        state[:WIDE] = jnp.zeros((WIDE, QROWS), F32)
        state[WIDE : WIDE + 8] = jnp.full((8, QROWS), FLOOR, F32)
        state[WIDE + 8 :] = jnp.zeros((8, QROWS), F32)
    else:
        state[...] = refs[-4][...]
    z, core, xh = here_ref[0], here_ref[1], here_ref[2]
    q_start = (xh * NZ + z) * QROWS
    q_last = q_start + QROWS - 1
    q_pos = q_start + lax.broadcasted_iota(jnp.int32, (1, QROWS), 1)
    doc_start = jnp.zeros((1, QROWS), jnp.int32)
    low, high, end = jnp.int32(0), jnp.int32(0), jnp.int32(0)
    for i in range(len_ref.shape[0]):
        end = end + len_ref[i]
        doc_start = jnp.where(q_pos >= end, end, doc_start)
        low = jnp.where(q_start >= end, end, low)
        high = jnp.where(q_last >= end, end, high)
    scale = math.log2(math.e) / math.sqrt(HD)

    def visit(slot, k_start, partial):
        keys = held[slot, :ROWS]
        values = held[slot, ROWS:].T
        if partial:
            k_pos = k_start + lax.broadcasted_iota(jnp.int32, (ROWS, QROWS), 0)
            allowed = (k_pos >= doc_start) & (k_pos <= q_pos)
        for h in range(HEADS):
            rows = slice(h * HD, (h + 1) * HD)
            scores = scale * lax.dot_general(keys, q_ref[:, rows], NEG, preferred_element_type=F32)
            if partial:
                scores = jnp.where(allowed, scores, MASKED)
            old = state[WIDE + h : WIDE + h + 1]
            new = jnp.maximum(old, jnp.max(scores, axis=0, keepdims=True))
            fix = jnp.exp2(old - new)
            weights = jnp.exp2(scores - new)
            state[WIDE + h : WIDE + h + 1] = new
            total = slice(WIDE + 8 + h, WIDE + 9 + h)
            state[total] = state[total] * fix + jnp.sum(weights, axis=0, keepdims=True)
            mixed = jnp.dot(values, weights.astype(BF16), preferred_element_type=F32)
            state[rows] = state[rows] * fix + mixed

    count = jnp.int32(0)
    for operand, block, offset, other in visits:
        plane = xh ^ 1 if other else xh
        k_start = (plane * NZ + ((z + NZ - offset) & (NZ - 1))) * QROWS + core * ROWS
        needed = (k_start + ROWS > low) & (k_start <= q_last)

        @pl.when(needed)
        def _():
            held[count] = refs[operand][block * QROWS : (block + 1) * QROWS]
            starts[count] = k_start

        count = count + needed.astype(jnp.int32)

    @pl.loop(0, count)
    def _(slot):
        k_start = starts[slot]
        whole = (k_start >= high) & (k_start + ROWS <= q_start + 1)
        pl.when(whole)(functools.partial(visit, slot, k_start, False))
        pl.when(jnp.logical_not(whole))(functools.partial(visit, slot, k_start, True))


def attend(here, lengths, q, visits, operands, state):
    smem = pl.BlockSpec(memory_space=pltpu.SMEM)
    vmem = pl.BlockSpec(memory_space=pltpu.VMEM)
    specs = [smem, smem, vmem] + [vmem] * len(operands)
    aliases = {}
    if state is not None:
        aliases = {len(specs): 0}
        operands = operands + [state]
        specs = specs + [vmem]
    pairs = (len(visits) + 1) // 2 * QROWS * ROWS * HEADS
    return pl.pallas_call(
        functools.partial(attend_kernel, visits, state is None),
        out_shape=jax.ShapeDtypeStruct((STATE, QROWS), F32),
        in_specs=specs,
        out_specs=vmem,
        scratch_shapes=[
            pltpu.VMEM((len(visits), QROWS, HD), BF16),
            pltpu.SMEM((len(visits),), jnp.int32),
        ],
        input_output_aliases=aliases,
        cost_estimate=pl.CostEstimate(
            flops=pairs * HD * COST, bytes_accessed=STATE * QROWS * COST, transcendentals=pairs
        ),
        compiler_params=pltpu.CompilerParams(vmem_limit_bytes=VMEM),
    )(here, lengths, q, *operands)


def merge_kernel(here_ref, mine_ref, other_ref, out_ref, a_ref, full):
    for h in range(HEADS):
        rows = slice(h * HD, (h + 1) * HD)
        top = slice(WIDE + h, WIDE + h + 1)
        total = slice(WIDE + 8 + h, WIDE + 9 + h)
        m = jnp.maximum(mine_ref[top], other_ref[top])
        mine, other = jnp.exp2(mine_ref[top] - m), jnp.exp2(other_ref[top] - m)
        den = mine * mine_ref[total] + other * other_ref[total]
        mixed = (mine_ref[rows] * mine + other_ref[rows] * other) / den
        full[:, rows] = mixed.T
    own = full[pl.ds(pl.multiple_of(here_ref[1] * ROWS, ROWS), ROWS)]
    out_ref[...] = own
    a_ref[...] = own.astype(BF16)


def merge(here, mine, other):
    vmem = pl.BlockSpec(memory_space=pltpu.VMEM)
    return pl.pallas_call(
        merge_kernel,
        out_shape=(
            jax.ShapeDtypeStruct((ROWS, WIDE), F32),
            jax.ShapeDtypeStruct((ROWS, WIDE), BF16),
        ),
        in_specs=[pl.BlockSpec(memory_space=pltpu.SMEM), vmem, vmem],
        out_specs=(vmem, vmem),
        scratch_shapes=[pltpu.VMEM((QROWS, WIDE), F32)],
        cost_estimate=pl.CostEstimate(
            flops=QROWS * WIDE * 100, bytes_accessed=STATE * QROWS * 12, transcendentals=QROWS * 16
        ),
        compiler_params=pltpu.CompilerParams(vmem_limit_bytes=VMEM),
    )(here, mine, other)


def project_kernel(here_ref, own_ref, other_ref, a_ref, out_ref):
    core, xh = here_ref[1], here_ref[2]
    k = lax.broadcasted_iota(jnp.int32, (DEEP, DEEP), 0)
    g = lax.broadcasted_iota(jnp.int32, (DEEP, DEEP), 1)
    row = g & (HD - 1)
    d = (xh ^ ((row >> 1) & 1)) * (NZ * 4) + (row >> 3) * 4 + (core ^ (g >> 7)) * 2 + (row & 1)
    match = ((k & (HD - 1)) == d) & (((row >> 2) & 1) == (k >> 7))
    perm = jnp.where(match, 1.0, 0.0).astype(BF16)
    total = jnp.zeros((ROWS, WIDE), F32)
    for y in range(NY):
        for h in range(HEADS):
            heads = slice(h * HD, (h + 1) * HD)
            columns = slice((y * HEADS + h) * WIDE, (y * HEADS + h + 1) * WIDE)
            both = jnp.concatenate([a_ref[y * NX + x, :, heads] for x in range(NX)], axis=1)
            moved = jnp.dot(both, perm, preferred_element_type=F32).astype(BF16)
            weight = jnp.concatenate([own_ref[:, columns], other_ref[:, columns]], axis=0)
            total += jnp.dot(moved, weight, preferred_element_type=F32)
    out_ref[...] = total


def project(here, weights, a):
    vmem = pl.BlockSpec(memory_space=pltpu.VMEM)
    return pl.pallas_call(
        project_kernel,
        out_shape=jax.ShapeDtypeStruct((ROWS, WIDE), F32),
        in_specs=[pl.BlockSpec(memory_space=pltpu.SMEM), vmem, vmem, vmem],
        out_specs=vmem,
        cost_estimate=pl.CostEstimate(
            flops=2 * NY * ROWS * DEEP * HEADS * (WIDE + DEEP),
            bytes_accessed=DEEP * NY * HEADS * WIDE * 2,
            transcendentals=0,
        ),
        compiler_params=pltpu.CompilerParams(vmem_limit_bytes=VMEM),
    )(here, *weights, a)


def swap(value, axis):
    return lax.ppermute(value, axis, [(0, 1), (1, 0)])


def ring(value, steps):
    return lax.ppermute(value, "z", [(i, (i + steps) % NZ) for i in range(NZ)])


def split_kernel(after_ref, weight_ref, out_ref):
    for j in range(NY * NX):
        for h in range(HEADS):
            out_ref[j, :, h * WIDE : (h + 1) * WIDE] = weight_ref[h, :, j * WIDE : (j + 1) * WIDE]


def stack_kernel(mine_ref, other_ref, out_ref):
    for e in range(NX):
        for rel, ref in enumerate((mine_ref, other_ref)):
            row = e * 4 + rel * 2
            for y in range(NY):
                lanes = slice(y * HEADS * WIDE, (y + 1) * HEADS * WIDE)
                out_ref[row : row + 2, lanes] = ref[y * NX + e]


def pass_kernel(*refs):
    pass


def behind(value, *after):
    whole = pl.BlockSpec(memory_space=pl.ANY)
    return pl.pallas_call(
        pass_kernel,
        out_shape=jax.ShapeDtypeStruct(value.shape, value.dtype),
        in_specs=[whole] * (1 + len(after)),
        out_specs=whole,
        input_output_aliases={0: 0},
    )(value, *after)


def split_weight(out_weight, after):
    whole = pl.BlockSpec(memory_space=pl.ANY)
    vmem = pl.BlockSpec(memory_space=pltpu.VMEM)
    split = pl.pallas_call(
        split_kernel,
        out_shape=jax.ShapeDtypeStruct((NY * NX, 2, HEADS * WIDE), BF16),
        in_specs=[whole, vmem],
        out_specs=vmem,
    )(after, out_weight)
    return lax.all_to_all(split, "tp", 0, 0)


def gather_weight(split):
    vmem = pl.BlockSpec(memory_space=pltpu.VMEM)
    rows = pl.pallas_call(
        stack_kernel,
        out_shape=jax.ShapeDtypeStruct((8, NY * HEADS * WIDE), BF16),
        in_specs=[vmem, vmem],
        out_specs=vmem,
    )(split, swap(split, "xh"))
    return lax.all_gather(rows, "z", axis=0, tiled=True)


def body(queries, keys, values, doc_lengths, out_weight):
    xh, z, core = (lax.axis_index(name) for name in ("xh", "z", "core"))
    here = jnp.stack([z, core, xh]).astype(jnp.int32)
    own = jnp.concatenate([keys, values], axis=0)
    pair = jnp.concatenate([own, swap(own, "xh")], axis=0)
    other_q = swap(queries, "core")
    q = jnp.where(core == 0, jnp.concatenate([queries, other_q]), jnp.concatenate([other_q, queries]))
    up, down = [pair], [pair]
    far = NZ // 2
    for _ in range(1, far):
        up.append(ring(up[-1], 1))
        down.append(ring(down[-1], -1))
    last = [ring(up[-1][:QROWS], 1), ring(down[-1][QROWS:], -1)]
    split = split_weight(out_weight, own)

    state = attend(here, doc_lengths, q, [(0, 0, 0, False), (0, 1, 0, True)], [pair], None)
    weight = gather_weight(behind(split, state))
    for s in range(1, far):
        visits = [(0, 0, s, False), (0, 1, s, True), (1, 0, -s, False), (1, 1, -s, True)]
        state = attend(here, doc_lengths, q, visits, [up[s], down[s]], state)
    state = attend(here, doc_lengths, q, [(0, 0, far, False), (1, 0, far, True)], last, state)
    attended, a = merge(here, state, swap(state, "core"))

    weight = behind(weight, a)
    sources = lax.all_to_all(jnp.broadcast_to(a[None], (NY * NX, ROWS, WIDE)), "tp", 0, 0)
    projected = project(here, (weight, swap(weight, "core")), sources)
    return (attended, projected)


def solution(mesh):
    fine = Mesh(mesh.devices.reshape(XH, NZ, NC, NY * NX), ("xh", "z", "core", "tp"))
    ctx = ("xh", "z", "core")
    in_specs = (P(ctx, "tp"), P(ctx, "tp"), P(ctx, "tp"), P(), P("tp", ctx, None))
    out_specs = (P(ctx, "tp"), P(ctx, "tp"))
    return jax.shard_map(body, mesh=fine, in_specs=in_specs, out_specs=out_specs, check_vma=False)
```

```python
import functools
import math

import jax
import jax.numpy as jnp
from jax import lax
from jax.experimental import pallas as pl
from jax.experimental.pallas import tpu as pltpu
from jax.sharding import Mesh, PartitionSpec as P

HD = 128
XH, NZ, NC, NY, NX = 2, 16, 2, 4, 2
ROWS = 224
QROWS = NC * ROWS
HEADS = 5
WIDE = HEADS * HD
STATE = WIDE + 16
DEEP = 2 * HD
COST = 64
FLOOR = -1e29
MASKED = -1e30
NEG = (((1,), (1,)), ((), ()))
VMEM = 40 * 1024 * 1024
F32 = jnp.float32
BF16 = jnp.bfloat16


def attend_kernel(visits, first, here_ref, len_ref, q_ref, *refs):
    held, starts, state = refs[-2], refs[-1], refs[-3]
    if first:
        state[:WIDE] = jnp.zeros((WIDE, QROWS), F32)
        state[WIDE : WIDE + 8] = jnp.full((8, QROWS), FLOOR, F32)
        state[WIDE + 8 :] = jnp.zeros((8, QROWS), F32)
    else:
        state[...] = refs[-4][...]
    z, core, xh = here_ref[0], here_ref[1], here_ref[2]
    q_start = (xh * NZ + z) * QROWS
    q_last = q_start + QROWS - 1
    q_pos = q_start + lax.broadcasted_iota(jnp.int32, (1, QROWS), 1)
    doc_start = jnp.zeros((1, QROWS), jnp.int32)
    low, high, end = jnp.int32(0), jnp.int32(0), jnp.int32(0)
    for i in range(len_ref.shape[0]):
        end = end + len_ref[i]
        doc_start = jnp.where(q_pos >= end, end, doc_start)
        low = jnp.where(q_start >= end, end, low)
        high = jnp.where(q_last >= end, end, high)
    scale = math.log2(math.e) / math.sqrt(HD)

    def visit(slot, k_start, partial):
        keys = held[slot, :ROWS]
        values = held[slot, ROWS:].T
        if partial:
            k_pos = k_start + lax.broadcasted_iota(jnp.int32, (ROWS, QROWS), 0)
            allowed = (k_pos >= doc_start) & (k_pos <= q_pos)
        for h in range(HEADS):
            rows = slice(h * HD, (h + 1) * HD)
            scores = scale * lax.dot_general(keys, q_ref[:, rows], NEG, preferred_element_type=F32)
            if partial:
                scores = jnp.where(allowed, scores, MASKED)
            old = state[WIDE + h : WIDE + h + 1]
            new = jnp.maximum(old, jnp.max(scores, axis=0, keepdims=True))
            fix = jnp.exp2(old - new)
            weights = jnp.exp2(scores - new)
            state[WIDE + h : WIDE + h + 1] = new
            total = slice(WIDE + 8 + h, WIDE + 9 + h)
            state[total] = state[total] * fix + jnp.sum(weights, axis=0, keepdims=True)
            mixed = jnp.dot(values, weights.astype(BF16), preferred_element_type=F32)
            state[rows] = state[rows] * fix + mixed

    count = jnp.int32(0)
    for operand, block, offset, other in visits:
        plane = xh ^ 1 if other else xh
        k_start = (plane * NZ + ((z + NZ - offset * (1 - 2 * core)) & (NZ - 1))) * QROWS + core * ROWS
        needed = (k_start + ROWS > low) & (k_start <= q_last)

        @pl.when(needed)
        def _():
            held[count] = refs[operand][block * QROWS : (block + 1) * QROWS]
            starts[count] = k_start

        count = count + needed.astype(jnp.int32)

    @pl.loop(0, count)
    def _(slot):
        k_start = starts[slot]
        whole = (k_start >= high) & (k_start + ROWS <= q_start + 1)
        pl.when(whole)(functools.partial(visit, slot, k_start, False))
        pl.when(jnp.logical_not(whole))(functools.partial(visit, slot, k_start, True))


def attend(here, lengths, q, visits, operands, state):
    smem = pl.BlockSpec(memory_space=pltpu.SMEM)
    vmem = pl.BlockSpec(memory_space=pltpu.VMEM)
    specs = [smem, smem, vmem] + [vmem] * len(operands)
    aliases = {}
    if state is not None:
        aliases = {len(specs): 0}
        operands = operands + [state]
        specs = specs + [vmem]
    pairs = (len(visits) + 1) // 2 * QROWS * ROWS * HEADS
    return pl.pallas_call(
        functools.partial(attend_kernel, visits, state is None),
        out_shape=jax.ShapeDtypeStruct((STATE, QROWS), F32),
        in_specs=specs,
        out_specs=vmem,
        scratch_shapes=[
            pltpu.VMEM((len(visits), QROWS, HD), BF16),
            pltpu.SMEM((len(visits),), jnp.int32),
        ],
        input_output_aliases=aliases,
        cost_estimate=pl.CostEstimate(
            flops=pairs * HD * COST, bytes_accessed=STATE * QROWS * COST, transcendentals=pairs
        ),
        compiler_params=pltpu.CompilerParams(vmem_limit_bytes=VMEM),
    )(here, lengths, q, *operands)


def merge_kernel(here_ref, mine_ref, other_ref, out_ref, a_ref, full):
    for h in range(HEADS):
        rows = slice(h * HD, (h + 1) * HD)
        top = slice(WIDE + h, WIDE + h + 1)
        total = slice(WIDE + 8 + h, WIDE + 9 + h)
        m = jnp.maximum(mine_ref[top], other_ref[top])
        mine, other = jnp.exp2(mine_ref[top] - m), jnp.exp2(other_ref[top] - m)
        den = mine * mine_ref[total] + other * other_ref[total]
        mixed = (mine_ref[rows] * mine + other_ref[rows] * other) / den
        full[:, rows] = mixed.T
    own = full[pl.ds(pl.multiple_of(here_ref[1] * ROWS, ROWS), ROWS)]
    out_ref[...] = own
    a_ref[...] = own.astype(BF16)


def merge(here, mine, other):
    vmem = pl.BlockSpec(memory_space=pltpu.VMEM)
    return pl.pallas_call(
        merge_kernel,
        out_shape=(
            jax.ShapeDtypeStruct((ROWS, WIDE), F32),
            jax.ShapeDtypeStruct((ROWS, WIDE), BF16),
        ),
        in_specs=[pl.BlockSpec(memory_space=pltpu.SMEM), vmem, vmem],
        out_specs=(vmem, vmem),
        scratch_shapes=[pltpu.VMEM((QROWS, WIDE), F32)],
        cost_estimate=pl.CostEstimate(
            flops=QROWS * WIDE * 100, bytes_accessed=STATE * QROWS * 12, transcendentals=QROWS * 16
        ),
        compiler_params=pltpu.CompilerParams(vmem_limit_bytes=VMEM),
    )(here, mine, other)


def project_kernel(first, here_ref, near_ref, far_ref, own_ref, other_ref, *refs):
    core, xh, xl = here_ref[2], here_ref[3], here_ref[4]
    k = lax.broadcasted_iota(jnp.int32, (DEEP, DEEP), 0)
    g = lax.broadcasted_iota(jnp.int32, (DEEP, DEEP), 1)
    source_core = core ^ (g >> 7)
    row = g & (HD - 1)
    d = (xh ^ ((row >> 1) & 1)) * (NZ * 4) + (row >> 3) * 4 + source_core * 2 + (row & 1)
    source_x = xl ^ (k >> 7)
    match = ((k & (HD - 1)) == d) & (((row >> 2) & 1) == source_x)
    perm = jnp.where(match, 1.0, 0.0).astype(BF16)
    total = jnp.zeros((ROWS, WIDE), F32) if first else refs[0][...]
    for h in range(HEADS):
        heads = slice(h * HD, (h + 1) * HD)
        columns = slice(h * WIDE, (h + 1) * WIDE)
        both = jnp.concatenate([near_ref[:, heads], far_ref[:, heads]], axis=1)
        moved = jnp.dot(both, perm, preferred_element_type=F32).astype(BF16)
        weight = jnp.concatenate([own_ref[:, columns], other_ref[:, columns]], axis=0)
        total += jnp.dot(moved, weight, preferred_element_type=F32)
    refs[-1][...] = total


def project(where, near, far, weights, total):
    block = pl.BlockSpec((ROWS, WIDE), lambda i, w: (0, 0))
    weight = pl.BlockSpec((HD, HEADS * WIDE), lambda i, w: (0, w[0]))
    totals = [] if total is None else [total]
    return pl.pallas_call(
        functools.partial(project_kernel, total is None),
        grid_spec=pltpu.PrefetchScalarGridSpec(
            num_scalar_prefetch=1,
            grid=(1,),
            in_specs=[block, block, weight, weight] + [block] * len(totals),
            out_specs=block,
        ),
        out_shape=jax.ShapeDtypeStruct((ROWS, WIDE), F32),
        cost_estimate=pl.CostEstimate(
            flops=2 * ROWS * DEEP * HEADS * (WIDE + DEEP),
            bytes_accessed=DEEP * HEADS * WIDE * 2,
            transcendentals=0,
        ),
        compiler_params=pltpu.CompilerParams(vmem_limit_bytes=VMEM),
    )(where, near, far, *weights, *totals)


def swap(value, axis):
    return lax.ppermute(value, axis, [(0, 1), (1, 0)])


def ring(value, steps):
    perm = [(i * NC + c, (i + steps * (1 - 2 * c)) % NZ * NC + c) for i in range(NZ) for c in range(NC)]
    return lax.ppermute(value, ("z", "core"), perm)


def hop(block, dy, dx):
    perm = [
        (sy * NX + sx, (sy + dy) % NY * NX + (sx ^ dx)) for sy in range(NY) for sx in range(NX)
    ]
    return lax.ppermute(block, "tp", perm)


def split_kernel(after_ref, weight_ref, out_ref):
    for j in range(NY * NX):
        for h in range(HEADS):
            out_ref[j, :, h * WIDE : (h + 1) * WIDE] = weight_ref[h, :, j * WIDE : (j + 1) * WIDE]


def stack_kernel(mine_ref, other_ref, out_ref):
    for e in range(NX):
        for rel, ref in enumerate((mine_ref, other_ref)):
            row = e * 4 + rel * 2
            for y in range(NY):
                lanes = slice(y * HEADS * WIDE, (y + 1) * HEADS * WIDE)
                out_ref[row : row + 2, lanes] = ref[y * NX + e]


def pass_kernel(*refs):
    pass


def behind(value, *after):
    whole = pl.BlockSpec(memory_space=pl.ANY)
    return pl.pallas_call(
        pass_kernel,
        out_shape=jax.ShapeDtypeStruct(value.shape, value.dtype),
        in_specs=[whole] * (1 + len(after)),
        out_specs=whole,
        input_output_aliases={0: 0},
    )(value, *after)


def split_weight(out_weight, after):
    whole = pl.BlockSpec(memory_space=pl.ANY)
    vmem = pl.BlockSpec(memory_space=pltpu.VMEM)
    split = pl.pallas_call(
        split_kernel,
        out_shape=jax.ShapeDtypeStruct((NY * NX, 2, HEADS * WIDE), BF16),
        in_specs=[whole, vmem],
        out_specs=vmem,
    )(after, out_weight)
    return lax.all_to_all(split, "tp", 0, 0)


def gather_weight(split):
    vmem = pl.BlockSpec(memory_space=pltpu.VMEM)
    rows = pl.pallas_call(
        stack_kernel,
        out_shape=jax.ShapeDtypeStruct((8, NY * HEADS * WIDE), BF16),
        in_specs=[vmem, vmem],
        out_specs=vmem,
    )(split, swap(split, "xh"))
    return lax.all_gather(rows, "z", axis=0, tiled=True)


def body(queries, keys, values, doc_lengths, out_weight):
    xh, z, core, tp = (lax.axis_index(name) for name in ("xh", "z", "core", "tp"))
    y, xl = tp // NX, tp % NX
    here = jnp.stack([z, core, xh]).astype(jnp.int32)
    own = jnp.concatenate([keys, values], axis=0)
    pair = jnp.concatenate([own, swap(own, "xh")], axis=0)
    other_q = swap(queries, "core")
    q = jnp.where(core == 0, jnp.concatenate([queries, other_q]), jnp.concatenate([other_q, queries]))
    up, down = [pair], [pair]
    far = NZ // 2
    for _ in range(1, far):
        up.append(ring(up[-1], 1))
        down.append(ring(down[-1], -1))
    last = [ring(up[-1][:QROWS], 1), ring(down[-1][QROWS:], -1)]
    split = split_weight(out_weight, own)

    state = attend(here, doc_lengths, q, [(0, 0, 0, False), (0, 1, 0, True)], [pair], None)
    weight = gather_weight(behind(split, state))
    for s in range(1, far):
        visits = [(0, 0, s, False), (0, 1, s, True), (1, 0, -s, False), (1, 1, -s, True)]
        state = attend(here, doc_lengths, q, visits, [up[s], down[s]], state)
    state = attend(here, doc_lengths, q, [(0, 0, far, False), (1, 0, far, True)], last, state)
    attended, a = merge(here, state, swap(state, "core"))

    weight = behind(weight, a)
    weights = (weight, swap(weight, "core"))
    below, above = hop(a, 1, 0), hop(a, -1, 0)
    across_below, across_above, across = hop(a, 1, 1), hop(a, -1, 1), hop(a, 0, 1)
    two, across_two = hop(below, 1, 0), hop(across_above, -1, 0)
    projected = None
    for dy, near, far in (
        (0, a, across),
        (-1, below, across_below),
        (1, above, across_above),
        (2, two, across_two),
    ):
        where = jnp.stack([(y + dy + NY) % NY, z, core, xh, xl]).astype(jnp.int32)
        projected = project(where, near, far, weights, projected)
    return (attended, projected)


def solution(mesh):
    fine = Mesh(mesh.devices.reshape(XH, NZ, NC, NY * NX), ("xh", "z", "core", "tp"))
    ctx = ("xh", "z", "core")
    in_specs = (P(ctx, "tp"), P(ctx, "tp"), P(ctx, "tp"), P(), P("tp", ctx, None))
    out_specs = (P(ctx, "tp"), P(ctx, "tp"))
    return jax.shard_map(body, mesh=fine, in_specs=in_specs, out_specs=out_specs, check_vma=False)
```

```python
import functools
import math

import jax
import jax.numpy as jnp
from jax import lax
from jax.experimental import pallas as pl
from jax.experimental.pallas import tpu as pltpu
from jax.sharding import Mesh, PartitionSpec as P

HD = 128
XH, NZ, NC, NY, NX = 2, 16, 2, 4, 2
ROWS = 224
QROWS = NC * ROWS
HEADS = 5
WIDE = HEADS * HD
STATE = WIDE + 16
DEEP = 2 * HD
COST = 64
FLOOR = -1e29
MASKED = -1e30
NEG = (((1,), (1,)), ((), ()))
VMEM = 40 * 1024 * 1024
F32 = jnp.float32
BF16 = jnp.bfloat16


def attend_kernel(visits, first, here_ref, len_ref, q_ref, *refs):
    held, starts, state = refs[-2], refs[-1], refs[-3]
    if first:
        state[:WIDE] = jnp.zeros((WIDE, QROWS), F32)
        state[WIDE : WIDE + 8] = jnp.full((8, QROWS), FLOOR, F32)
        state[WIDE + 8 :] = jnp.zeros((8, QROWS), F32)
    else:
        state[...] = refs[-4][...]
    z, core, xh = here_ref[0], here_ref[1], here_ref[2]
    q_start = (xh * NZ + z) * QROWS
    q_last = q_start + QROWS - 1
    q_pos = q_start + lax.broadcasted_iota(jnp.int32, (1, QROWS), 1)
    doc_start = jnp.zeros((1, QROWS), jnp.int32)
    low, high, end = jnp.int32(0), jnp.int32(0), jnp.int32(0)
    for i in range(len_ref.shape[0]):
        end = end + len_ref[i]
        doc_start = jnp.where(q_pos >= end, end, doc_start)
        low = jnp.where(q_start >= end, end, low)
        high = jnp.where(q_last >= end, end, high)
    scale = math.log2(math.e) / math.sqrt(HD)

    def visit(slot, k_start, partial):
        keys = held[slot, :ROWS]
        values = held[slot, ROWS:].T
        if partial:
            k_pos = k_start + lax.broadcasted_iota(jnp.int32, (ROWS, QROWS), 0)
            allowed = (k_pos >= doc_start) & (k_pos <= q_pos)
        for h in range(HEADS):
            rows = slice(h * HD, (h + 1) * HD)
            scores = scale * lax.dot_general(keys, q_ref[:, rows], NEG, preferred_element_type=F32)
            if partial:
                scores = jnp.where(allowed, scores, MASKED)
            old = state[WIDE + h : WIDE + h + 1]
            new = jnp.maximum(old, jnp.max(scores, axis=0, keepdims=True))
            fix = jnp.exp2(old - new)
            weights = jnp.exp2(scores - new)
            state[WIDE + h : WIDE + h + 1] = new
            total = slice(WIDE + 8 + h, WIDE + 9 + h)
            state[total] = state[total] * fix + jnp.sum(weights, axis=0, keepdims=True)
            mixed = jnp.dot(values, weights.astype(BF16), preferred_element_type=F32)
            state[rows] = state[rows] * fix + mixed

    count = jnp.int32(0)
    for operand, block, offset, other in visits:
        plane = xh ^ 1 if other else xh
        k_start = (plane * NZ + ((z + NZ - offset) & (NZ - 1))) * QROWS + core * ROWS
        needed = (k_start + ROWS > low) & (k_start <= q_last)

        @pl.when(needed)
        def _():
            held[count] = refs[operand][block * QROWS : (block + 1) * QROWS]
            starts[count] = k_start

        count = count + needed.astype(jnp.int32)

    @pl.loop(0, count)
    def _(slot):
        k_start = starts[slot]
        whole = (k_start >= high) & (k_start + ROWS <= q_start + 1)
        pl.when(whole)(functools.partial(visit, slot, k_start, False))
        pl.when(jnp.logical_not(whole))(functools.partial(visit, slot, k_start, True))


def attend(here, lengths, q, visits, operands, state):
    smem = pl.BlockSpec(memory_space=pltpu.SMEM)
    vmem = pl.BlockSpec(memory_space=pltpu.VMEM)
    specs = [smem, smem, vmem] + [vmem] * len(operands)
    aliases = {}
    if state is not None:
        aliases = {len(specs): 0}
        operands = operands + [state]
        specs = specs + [vmem]
    pairs = (len(visits) + 1) // 2 * QROWS * ROWS * HEADS
    return pl.pallas_call(
        functools.partial(attend_kernel, visits, state is None),
        out_shape=jax.ShapeDtypeStruct((STATE, QROWS), F32),
        in_specs=specs,
        out_specs=vmem,
        scratch_shapes=[
            pltpu.VMEM((len(visits), QROWS, HD), BF16),
            pltpu.SMEM((len(visits),), jnp.int32),
        ],
        input_output_aliases=aliases,
        cost_estimate=pl.CostEstimate(
            flops=pairs * HD * COST, bytes_accessed=STATE * QROWS * COST, transcendentals=pairs
        ),
        compiler_params=pltpu.CompilerParams(vmem_limit_bytes=VMEM),
    )(here, lengths, q, *operands)


def merge_kernel(mine_ref, other_ref, out_ref, a_ref):
    for h in range(HEADS):
        rows = slice(h * HD, (h + 1) * HD)
        top = slice(WIDE + h, WIDE + h + 1)
        total = slice(WIDE + 8 + h, WIDE + 9 + h)
        m = jnp.maximum(mine_ref[top], other_ref[top])
        mine, other = jnp.exp2(mine_ref[top] - m), jnp.exp2(other_ref[top] - m)
        den = mine * mine_ref[total] + other * other_ref[total]
        mixed = (mine_ref[rows] * mine + other_ref[rows] * other) / den
        mixed = mixed.T
        out_ref[:, rows] = mixed
        a_ref[:, rows] = mixed.astype(BF16)


def merge(mine, other):
    vmem = pl.BlockSpec(memory_space=pltpu.VMEM)
    return pl.pallas_call(
        merge_kernel,
        out_shape=(
            jax.ShapeDtypeStruct((ROWS, WIDE), F32),
            jax.ShapeDtypeStruct((ROWS, WIDE), BF16),
        ),
        in_specs=[vmem, vmem],
        out_specs=(vmem, vmem),
        cost_estimate=pl.CostEstimate(
            flops=QROWS * WIDE * 100, bytes_accessed=STATE * QROWS * 12, transcendentals=QROWS * 16
        ),
        compiler_params=pltpu.CompilerParams(vmem_limit_bytes=VMEM),
    )(mine, other)


def project_kernel(here_ref, own_ref, other_ref, a_ref, out_ref):
    core, xh = here_ref[1], here_ref[2]
    k = lax.broadcasted_iota(jnp.int32, (DEEP, DEEP), 0)
    g = lax.broadcasted_iota(jnp.int32, (DEEP, DEEP), 1)
    row = g & (HD - 1)
    d = (xh ^ ((row >> 1) & 1)) * (NZ * 4) + (row >> 3) * 4 + (core ^ (g >> 7)) * 2 + (row & 1)
    match = ((k & (HD - 1)) == d) & (((row >> 2) & 1) == (k >> 7))
    perm = jnp.where(match, 1.0, 0.0).astype(BF16)
    total = jnp.zeros((ROWS, WIDE), F32)
    for y in range(NY):
        for h in range(HEADS):
            heads = slice(h * HD, (h + 1) * HD)
            columns = slice((y * HEADS + h) * WIDE, (y * HEADS + h + 1) * WIDE)
            both = jnp.concatenate([a_ref[y * NX + x, :, heads] for x in range(NX)], axis=1)
            moved = jnp.dot(both, perm, preferred_element_type=F32).astype(BF16)
            weight = jnp.concatenate([own_ref[:, columns], other_ref[:, columns]], axis=0)
            total += jnp.dot(moved, weight, preferred_element_type=F32)
    out_ref[...] = total


def project(here, weights, a):
    vmem = pl.BlockSpec(memory_space=pltpu.VMEM)
    return pl.pallas_call(
        project_kernel,
        out_shape=jax.ShapeDtypeStruct((ROWS, WIDE), F32),
        in_specs=[pl.BlockSpec(memory_space=pltpu.SMEM), vmem, vmem, vmem],
        out_specs=vmem,
        cost_estimate=pl.CostEstimate(
            flops=2 * NY * ROWS * DEEP * HEADS * (WIDE + DEEP),
            bytes_accessed=DEEP * NY * HEADS * WIDE * 2,
            transcendentals=0,
        ),
        compiler_params=pltpu.CompilerParams(vmem_limit_bytes=VMEM),
    )(here, *weights, a)


def swap(value, axis):
    return lax.ppermute(value, axis, [(0, 1), (1, 0)])


def ring(value, steps):
    return lax.ppermute(value, "z", [(i, (i + steps) % NZ) for i in range(NZ)])


def split_kernel(after_ref, weight_ref, out_ref):
    for j in range(NY * NX):
        for h in range(HEADS):
            out_ref[j, :, h * WIDE : (h + 1) * WIDE] = weight_ref[h, :, j * WIDE : (j + 1) * WIDE]


def stack_kernel(mine_ref, other_ref, out_ref):
    for e in range(NX):
        for rel, ref in enumerate((mine_ref, other_ref)):
            row = e * 4 + rel * 2
            for y in range(NY):
                lanes = slice(y * HEADS * WIDE, (y + 1) * HEADS * WIDE)
                out_ref[row : row + 2, lanes] = ref[y * NX + e]


def pass_kernel(*refs):
    pass


def behind(value, *after):
    whole = pl.BlockSpec(memory_space=pl.ANY)
    return pl.pallas_call(
        pass_kernel,
        out_shape=jax.ShapeDtypeStruct(value.shape, value.dtype),
        in_specs=[whole] * (1 + len(after)),
        out_specs=whole,
        input_output_aliases={0: 0},
    )(value, *after)


def split_weight(out_weight, after):
    whole = pl.BlockSpec(memory_space=pl.ANY)
    vmem = pl.BlockSpec(memory_space=pltpu.VMEM)
    split = pl.pallas_call(
        split_kernel,
        out_shape=jax.ShapeDtypeStruct((NY * NX, 2, HEADS * WIDE), BF16),
        in_specs=[whole, vmem],
        out_specs=vmem,
    )(after, out_weight)
    return lax.all_to_all(split, "tp", 0, 0)


def gather_weight(split):
    vmem = pl.BlockSpec(memory_space=pltpu.VMEM)
    rows = pl.pallas_call(
        stack_kernel,
        out_shape=jax.ShapeDtypeStruct((8, NY * HEADS * WIDE), BF16),
        in_specs=[vmem, vmem],
        out_specs=vmem,
    )(split, swap(split, "xh"))
    return lax.all_gather(rows, "z", axis=0, tiled=True)


def body(queries, keys, values, doc_lengths, out_weight):
    xh, z, core = (lax.axis_index(name) for name in ("xh", "z", "core"))
    here = jnp.stack([z, core, xh]).astype(jnp.int32)
    own = jnp.concatenate([keys, values], axis=0)
    pair = jnp.concatenate([own, swap(own, "xh")], axis=0)
    other_q = swap(queries, "core")
    q = jnp.where(core == 0, jnp.concatenate([queries, other_q]), jnp.concatenate([other_q, queries]))
    up, down = [pair], [pair]
    far = NZ // 2
    for _ in range(1, far):
        up.append(ring(up[-1], 1))
        down.append(ring(down[-1], -1))
    last = [ring(up[-1][:QROWS], 1), ring(down[-1][QROWS:], -1)]
    split = split_weight(out_weight, own)

    state = attend(here, doc_lengths, q, [(0, 0, 0, False), (0, 1, 0, True)], [pair], None)
    weight = gather_weight(behind(split, state))
    for s in range(1, far):
        visits = [(0, 0, s, False), (0, 1, s, True), (1, 0, -s, False), (1, 1, -s, True)]
        state = attend(here, doc_lengths, q, visits, [up[s], down[s]], state)
    state = attend(here, doc_lengths, q, [(0, 0, far, False), (1, 0, far, True)], last, state)
    low, high = state[:, :ROWS], state[:, ROWS:]
    sent, kept = jnp.where(core == 0, high, low), jnp.where(core == 0, low, high)
    attended, a = merge(kept, swap(sent, "core"))

    weight = behind(weight, a)
    sources = lax.all_to_all(jnp.broadcast_to(a[None], (NY * NX, ROWS, WIDE)), "tp", 0, 0)
    projected = project(here, (weight, swap(weight, "core")), sources)
    return (attended, projected)


def solution(mesh):
    fine = Mesh(mesh.devices.reshape(XH, NZ, NC, NY * NX), ("xh", "z", "core", "tp"))
    ctx = ("xh", "z", "core")
    in_specs = (P(ctx, "tp"), P(ctx, "tp"), P(ctx, "tp"), P(), P("tp", ctx, None))
    out_specs = (P(ctx, "tp"), P(ctx, "tp"))
    return jax.shard_map(body, mesh=fine, in_specs=in_specs, out_specs=out_specs, check_vma=False)
```

```python
import functools
import math

import jax
import jax.numpy as jnp
from jax import lax
from jax.experimental import pallas as pl
from jax.experimental.pallas import tpu as pltpu
from jax.sharding import Mesh, PartitionSpec as P

HD = 128
XH, NZ, NC, NY, NX = 2, 16, 2, 4, 2
ROWS = 224
QROWS = NC * ROWS
HEADS = 5
WIDE = HEADS * HD
STATE = WIDE + 16
DEEP = 2 * HD
COST = 64
FLOOR = -1e29
MASKED = -1e30
NEG = (((1,), (1,)), ((), ()))
VMEM = 40 * 1024 * 1024
F32 = jnp.float32
BF16 = jnp.bfloat16


def attend_kernel(visits, first, here_ref, len_ref, q_ref, *refs):
    held, starts, state = refs[-2], refs[-1], refs[-3]
    if first:
        state[:WIDE] = jnp.zeros((WIDE, QROWS), F32)
        state[WIDE : WIDE + 8] = jnp.full((8, QROWS), FLOOR, F32)
        state[WIDE + 8 :] = jnp.zeros((8, QROWS), F32)
    else:
        state[...] = refs[-4][...]
    z, core, xh = here_ref[0], here_ref[1], here_ref[2]
    q_start = (xh * NZ + z) * QROWS
    q_last = q_start + QROWS - 1
    q_pos = q_start + lax.broadcasted_iota(jnp.int32, (1, QROWS), 1)
    doc_start = jnp.zeros((1, QROWS), jnp.int32)
    low, high, end = jnp.int32(0), jnp.int32(0), jnp.int32(0)
    for i in range(len_ref.shape[0]):
        end = end + len_ref[i]
        doc_start = jnp.where(q_pos >= end, end, doc_start)
        low = jnp.where(q_start >= end, end, low)
        high = jnp.where(q_last >= end, end, high)
    scale = math.log2(math.e) / math.sqrt(HD)

    def visit(slot, k_start, partial):
        keys = held[slot, :ROWS]
        values = held[slot, ROWS:].T
        if partial:
            k_pos = k_start + lax.broadcasted_iota(jnp.int32, (ROWS, QROWS), 0)
            allowed = (k_pos >= doc_start) & (k_pos <= q_pos)
        for h in range(HEADS):
            rows = slice(h * HD, (h + 1) * HD)
            scores = scale * lax.dot_general(keys, q_ref[:, rows], NEG, preferred_element_type=F32)
            if partial:
                scores = jnp.where(allowed, scores, MASKED)
            old = state[WIDE + h : WIDE + h + 1]
            new = jnp.maximum(old, jnp.max(scores, axis=0, keepdims=True))
            fix = jnp.exp2(old - new)
            weights = jnp.exp2(scores - new)
            state[WIDE + h : WIDE + h + 1] = new
            total = slice(WIDE + 8 + h, WIDE + 9 + h)
            state[total] = state[total] * fix + jnp.sum(weights, axis=0, keepdims=True)
            mixed = jnp.dot(values, weights.astype(BF16), preferred_element_type=F32)
            state[rows] = state[rows] * fix + mixed

    count = jnp.int32(0)
    for operand, block, offset, other in visits:
        plane = xh ^ 1 if other else xh
        k_start = (plane * NZ + ((z + NZ - offset) & (NZ - 1))) * QROWS + core * ROWS
        needed = (k_start + ROWS > low) & (k_start <= q_last)

        @pl.when(needed)
        def _():
            held[count] = refs[operand][block * QROWS : (block + 1) * QROWS]
            starts[count] = k_start

        count = count + needed.astype(jnp.int32)

    @pl.loop(0, count)
    def _(slot):
        k_start = starts[slot]
        whole = (k_start >= high) & (k_start + ROWS <= q_start + 1)
        pl.when(whole)(functools.partial(visit, slot, k_start, False))
        pl.when(jnp.logical_not(whole))(functools.partial(visit, slot, k_start, True))


def attend(here, lengths, q, visits, operands, state):
    smem = pl.BlockSpec(memory_space=pltpu.SMEM)
    vmem = pl.BlockSpec(memory_space=pltpu.VMEM)
    specs = [smem, smem, vmem] + [vmem] * len(operands)
    aliases = {}
    if state is not None:
        aliases = {len(specs): 0}
        operands = operands + [state]
        specs = specs + [vmem]
    pairs = (len(visits) + 1) // 2 * QROWS * ROWS * HEADS
    return pl.pallas_call(
        functools.partial(attend_kernel, visits, state is None),
        out_shape=jax.ShapeDtypeStruct((STATE, QROWS), F32),
        in_specs=specs,
        out_specs=vmem,
        scratch_shapes=[
            pltpu.VMEM((len(visits), QROWS, HD), BF16),
            pltpu.SMEM((len(visits),), jnp.int32),
        ],
        input_output_aliases=aliases,
        cost_estimate=pl.CostEstimate(
            flops=pairs * HD * COST, bytes_accessed=STATE * QROWS * COST, transcendentals=pairs
        ),
        compiler_params=pltpu.CompilerParams(vmem_limit_bytes=VMEM),
    )(here, lengths, q, *operands)


def merge_kernel(mine_ref, other_ref, out_ref, a_ref):
    for h in range(HEADS):
        rows = slice(h * HD, (h + 1) * HD)
        top = slice(WIDE + h, WIDE + h + 1)
        total = slice(WIDE + 8 + h, WIDE + 9 + h)
        m = jnp.maximum(mine_ref[top], other_ref[top])
        mine, other = jnp.exp2(mine_ref[top] - m), jnp.exp2(other_ref[top] - m)
        den = mine * mine_ref[total] + other * other_ref[total]
        mixed = (mine_ref[rows] * mine + other_ref[rows] * other) / den
        mixed = mixed.T
        out_ref[:, rows] = mixed
        a_ref[:, rows] = mixed.astype(BF16)


def merge(mine, other):
    vmem = pl.BlockSpec(memory_space=pltpu.VMEM)
    return pl.pallas_call(
        merge_kernel,
        out_shape=(
            jax.ShapeDtypeStruct((ROWS, WIDE), F32),
            jax.ShapeDtypeStruct((ROWS, WIDE), BF16),
        ),
        in_specs=[vmem, vmem],
        out_specs=(vmem, vmem),
        cost_estimate=pl.CostEstimate(
            flops=QROWS * WIDE * 100, bytes_accessed=STATE * QROWS * 12, transcendentals=QROWS * 16
        ),
        compiler_params=pltpu.CompilerParams(vmem_limit_bytes=VMEM),
    )(mine, other)


def project_kernel(here_ref, own_ref, other_ref, a_ref, out_ref):
    core, xh = here_ref[1], here_ref[2]
    k = lax.broadcasted_iota(jnp.int32, (DEEP, DEEP), 0)
    g = lax.broadcasted_iota(jnp.int32, (DEEP, DEEP), 1)
    row = g & (HD - 1)
    d = (xh ^ ((row >> 1) & 1)) * (NZ * 4) + (row >> 3) * 4 + (core ^ (g >> 7)) * 2 + (row & 1)
    match = ((k & (HD - 1)) == d) & (((row >> 2) & 1) == (k >> 7))
    perm = jnp.where(match, 1.0, 0.0).astype(BF16)
    total = jnp.zeros((ROWS, WIDE), F32)
    for y in range(NY):
        for h in range(HEADS):
            heads = slice(h * HD, (h + 1) * HD)
            columns = slice((y * HEADS + h) * WIDE, (y * HEADS + h + 1) * WIDE)
            both = jnp.concatenate([a_ref[y * NX + x, :, heads] for x in range(NX)], axis=1)
            moved = jnp.dot(both, perm, preferred_element_type=F32).astype(BF16)
            weight = jnp.concatenate([own_ref[:, columns], other_ref[:, columns]], axis=0)
            total += jnp.dot(moved, weight, preferred_element_type=F32)
    out_ref[...] = total


def project(here, weights, a):
    vmem = pl.BlockSpec(memory_space=pltpu.VMEM)
    return pl.pallas_call(
        project_kernel,
        out_shape=jax.ShapeDtypeStruct((ROWS, WIDE), F32),
        in_specs=[pl.BlockSpec(memory_space=pltpu.SMEM), vmem, vmem, vmem],
        out_specs=vmem,
        cost_estimate=pl.CostEstimate(
            flops=2 * NY * ROWS * DEEP * HEADS * (WIDE + DEEP),
            bytes_accessed=DEEP * NY * HEADS * WIDE * 2,
            transcendentals=0,
        ),
        compiler_params=pltpu.CompilerParams(vmem_limit_bytes=VMEM),
    )(here, *weights, a)


def swap(value, axis):
    return lax.ppermute(value, axis, [(0, 1), (1, 0)])


def ring(value, steps):
    return lax.ppermute(value, "z", [(i, (i + steps) % NZ) for i in range(NZ)])


def split_kernel(after_ref, weight_ref, out_ref):
    for j in range(NY * NX):
        for h in range(HEADS):
            out_ref[j, :, h * WIDE : (h + 1) * WIDE] = weight_ref[h, :, j * WIDE : (j + 1) * WIDE]


def stack_kernel(mine_ref, other_ref, out_ref):
    for e in range(NX):
        for rel, ref in enumerate((mine_ref, other_ref)):
            row = e * 4 + rel * 2
            for y in range(NY):
                lanes = slice(y * HEADS * WIDE, (y + 1) * HEADS * WIDE)
                out_ref[row : row + 2, lanes] = ref[y * NX + e]


def pass_kernel(*refs):
    pass


def behind(value, *after):
    whole = pl.BlockSpec(memory_space=pl.ANY)
    return pl.pallas_call(
        pass_kernel,
        out_shape=jax.ShapeDtypeStruct(value.shape, value.dtype),
        in_specs=[whole] * (1 + len(after)),
        out_specs=whole,
        input_output_aliases={0: 0},
    )(value, *after)


def split_weight(out_weight, after):
    whole = pl.BlockSpec(memory_space=pl.ANY)
    vmem = pl.BlockSpec(memory_space=pltpu.VMEM)
    split = pl.pallas_call(
        split_kernel,
        out_shape=jax.ShapeDtypeStruct((NY * NX, 2, HEADS * WIDE), BF16),
        in_specs=[whole, vmem],
        out_specs=vmem,
    )(after, out_weight)
    return lax.all_to_all(split, "tp", 0, 0)


def gather_weight(split):
    vmem = pl.BlockSpec(memory_space=pltpu.VMEM)
    rows = pl.pallas_call(
        stack_kernel,
        out_shape=jax.ShapeDtypeStruct((8, NY * HEADS * WIDE), BF16),
        in_specs=[vmem, vmem],
        out_specs=vmem,
    )(split, swap(split, "xh"))
    return lax.all_gather(rows, "z", axis=0, tiled=True)


def body(queries, keys, values, doc_lengths, out_weight):
    xh, z, core = (lax.axis_index(name) for name in ("xh", "z", "core"))
    here = jnp.stack([z, core, xh]).astype(jnp.int32)
    own = jnp.concatenate([keys, values], axis=0)
    pair = jnp.concatenate([own, swap(own, "xh")], axis=0)
    other_q = swap(queries, "core")
    q = jnp.where(core == 0, jnp.concatenate([queries, other_q]), jnp.concatenate([other_q, queries]))
    up, down = [pair], [pair]
    far = NZ // 2
    for _ in range(1, far):
        up.append(ring(up[-1], 1))
        down.append(ring(down[-1], -1))
    last = [ring(up[-1][:QROWS], 1), ring(down[-1][QROWS:], -1)]
    split = split_weight(out_weight, own)

    state = attend(here, doc_lengths, q, [(0, 0, 0, False), (0, 1, 0, True)], [pair], None)
    weight = gather_weight(behind(split, state))
    for s in range(1, far):
        visits = [(0, 0, s, False), (0, 1, s, True), (1, 0, -s, False), (1, 1, -s, True)]
        state = attend(here, doc_lengths, q, visits, [up[s], down[s]], state)
    state = attend(here, doc_lengths, q, [(0, 0, far, False), (1, 0, far, True)], last, state)
    low, high = state[:, :ROWS], state[:, ROWS:]
    sent, kept = jnp.where(core == 0, high, low), jnp.where(core == 0, low, high)
    attended, a = merge(kept, swap(sent, "core"))

    weight = behind(weight, state)
    sources = lax.all_to_all(jnp.broadcast_to(a[None], (NY * NX, ROWS, WIDE)), "tp", 0, 0)
    projected = project(here, (weight, swap(weight, "core")), sources)
    return (attended, projected)


def solution(mesh):
    fine = Mesh(mesh.devices.reshape(XH, NZ, NC, NY * NX), ("xh", "z", "core", "tp"))
    ctx = ("xh", "z", "core")
    in_specs = (P(ctx, "tp"), P(ctx, "tp"), P(ctx, "tp"), P(), P("tp", ctx, None))
    out_specs = (P(ctx, "tp"), P(ctx, "tp"))
    return jax.shard_map(body, mesh=fine, in_specs=in_specs, out_specs=out_specs, check_vma=False)
```
